768 devices in a mesh: group: 8 (over x, y_hi), replica: 96 (over y_lo, z, core).
Axes of the slice: x: 4, y: 8 (y_hi: 2, y_lo: 4; y = y_hi * 4 + y_lo), z: 12, core: 2. Of those that a mesh axis runs over, the one named last changes fastest.
Arguments:
- hidden_in: bfloat16 [98304, 4096], P(('group', 'replica')), may hold values from -40 to 40
- norm_gain: bfloat16 [4096], P('group'), may hold values from 0.099609375 to 1.8984375
- key_codes: bfloat16 [4096, 512], P('group'), may hold values from -4 to 4
- key_scales: bfloat16 [4096, 2], P('group'), may hold values from 0.0049743652 to 0.049804688
- key_cotangent: bfloat16 [98304, 512], P(('group', 'replica')), may hold values from -17 to 17
Outputs:
- keys_out: bfloat16 [98304, 512], P(('group', 'replica'))
- input_gradient: bfloat16 [98304, 4096], P(('group', 'replica'))
- weight_grad: bfloat16 [4096, 512], P('group')
- gain_gradient: float32 [4096], replicated
The draws below stay inside these ranges and needn't reach their ends.
All inputs are finite; a program needn't handle non-finite values.
Results may differ from the reference program's by a relative error of at most 0.017.
Values may be sent and summed in bfloat16 or wider, within the bound.
No kernel may reach another device: no remote copies, remote signals or barrier semaphores. Data moves between devices by JAX's collectives and lax.ppermute only.
A program may use at most 64 MiB of HBM per device.

```python
import math
import jax
import jax.numpy as jnp
from jax import lax

D = 4096
BLOCK = 256
TOK_DEV = 128
KEYS = 512
TOKENS = 98304
N_GROUP = 8
N_REPLICA = 96


def draw_hidden_in(key, part):
    key = jax.random.fold_in(key, 11)
    first, second = jax.random.split(key)
    rows = jnp.exp(jax.random.uniform(second, (TOKENS, 1), jnp.float32) * math.log(10.0))
    base = jnp.clip(jax.random.normal(first, (TOKENS, D), jnp.float32), -4.0, 4.0)
    return (base * rows).astype(jnp.bfloat16)


def draw_key_cotangent(key, part):
    key = jax.random.fold_in(key, 23)
    first = jax.random.fold_in(key, 0)
    position = jnp.arange(TOKENS, dtype=jnp.float32)[:, None] / TOKENS
    rising = 1.0 + 2.0 * position
    values = jnp.clip(jax.random.normal(first, (TOKENS, KEYS), jnp.float32), -4.0, 4.0) * rising
    return values.astype(jnp.bfloat16)


def block_levels(rng, shape, cuts, low, top_value):
    def one(dim, shards_of):
        steps = jax.random.uniform(jax.random.fold_in(jax.random.fold_in(rng, 6), dim), (shards_of,), jnp.float32, low / len(cuts), top_value / len(cuts))
        return jnp.repeat(jnp.exp(steps), shape[dim] // shards_of).reshape((-1,) + (1,) * (len(shape) - dim - 1))

    gain = one(*cuts[0])
    for cut in cuts[1:]:
        gain = gain * one(*cut)
    return gain


def bell_draw(key, dims, scale, bound, pieces=(), held_as=jnp.bfloat16):
    result = jax.random.normal(key, dims, jnp.float32) * scale
    if len(pieces) > 0:
        result = block_levels(key, dims, pieces, -0.22, 0.18) * result
    return jnp.clip(result, min=-bound, max=bound).astype(held_as)


def setup_inputs(seed: int = 0) -> dict:
    arg_keys = jax.random.split(jax.random.key(seed), 6)
    return {
        "hidden_in": draw_hidden_in(jax.random.fold_in(arg_keys[5], 71), 0),
        "norm_gain": jnp.clip(1.0 + 0.18 * jax.random.normal(arg_keys[1], (D,), jnp.float32), 0.099609375, 1.8984375).astype(jnp.bfloat16),
        "key_codes": bell_draw(arg_keys[2], (D, KEYS), 1.0, 4.0, ((0, 8),)),
        "key_scales": jnp.clip(jnp.exp(math.log(0.049804688) - 2.3038113 * jax.random.uniform(arg_keys[3], (D, KEYS // BLOCK), jnp.float32) ** block_levels(arg_keys[3], (D, KEYS // BLOCK), ((0, 8),), -0.2, 0.2)), 0.0049743652, 0.049804688).astype(jnp.bfloat16),
        "key_cotangent": draw_key_cotangent(jax.random.fold_in(arg_keys[5], 71), 0),
    }


def dequantize(codes, scales):
    rows = codes.shape[0]
    grouped = codes.astype(jnp.float32).reshape(rows, -1, BLOCK) * scales.astype(jnp.float32)[:, :, None]
    return grouped.reshape(rows, -1).astype(jnp.bfloat16)

def reference(hidden_in, norm_gain, key_codes, key_scales, key_cotangent):
    hidden_rows = hidden_in.astype(jnp.float32)
    inverse_norm = lax.rsqrt(lax.optimization_barrier(jnp.mean(hidden_rows * hidden_rows, axis=1, keepdims=True)) + 1e-05)
    unit_rows = hidden_rows * inverse_norm
    gain_vector = norm_gain.astype(jnp.float32)
    normalized_rows = (unit_rows * gain_vector).astype(jnp.bfloat16)
    weight = dequantize(key_codes, key_scales)
    keys_out = jnp.dot(normalized_rows, weight, preferred_element_type=jnp.float32).astype(jnp.bfloat16)
    normalized_gradient = jnp.dot(key_cotangent, weight.T, preferred_element_type=jnp.float32)
    unit_input_gradient = normalized_gradient * gain_vector
    input_gradient = (inverse_norm * (unit_input_gradient - unit_rows * lax.optimization_barrier(jnp.mean(unit_input_gradient * unit_rows, axis=1, keepdims=True)))).astype(jnp.bfloat16)
    devices_all = N_GROUP * N_REPLICA
    normed_blocks = normalized_rows.reshape(devices_all, TOK_DEV, D)
    cot_blocks = key_cotangent.reshape(devices_all, TOK_DEV, KEYS)

    def accumulate(total, pair):
        partial_value = jnp.dot(pair[0].T, pair[1], preferred_element_type=jnp.float32)
        rounded = lax.optimization_barrier(partial_value.astype(jnp.bfloat16))
        return (total + rounded.astype(jnp.float32), None)
    total, unused = lax.scan(accumulate, jnp.zeros((D, KEYS), jnp.float32), (normed_blocks, cot_blocks))
    scale_multiplier = 1.0 / jnp.sqrt(jnp.float32(TOKENS))
    weight_grad = (total * scale_multiplier).astype(jnp.bfloat16)
    gain_gradient = lax.optimization_barrier(jnp.sum(normalized_gradient * unit_rows, axis=0)) * scale_multiplier
    return (keys_out, input_gradient, weight_grad, gain_gradient)
```

```python
import jax
import jax.numpy as jnp
from jax import lax
from jax.sharding import Mesh
from jax.sharding import PartitionSpec as P

F32 = jnp.float32
BF16 = jnp.bfloat16


def spread(value, axes, size):
    copies = jnp.broadcast_to(value[None], (size,) + value.shape)
    return lax.all_to_all(copies, axes, 0, 0)


def by_core(own, other):
    first = lax.axis_index("c") == 0
    return jnp.where(first, own, other), jnp.where(first, other, own)


def body(hidden_in, norm_gain, key_codes, key_scales, key_cotangent):
    nx, nh, nl, nz, nc = (lax.axis_size(a) for a in ("x", "yh", "yl", "z", "c"))
    tok, width = hidden_in.shape
    rows, cols = key_codes.shape
    block = cols // key_scales.shape[1]
    total_tokens = tok * nx * nh * nl * nz * nc
    half = rows // nc
    core = lax.axis_index("c")
    swap_c = [(0, 1), (1, 0)]

    gain = norm_gain.astype(F32)[:, None]
    scales = jnp.repeat(key_scales.astype(F32), block, axis=1)
    scaled = key_codes.astype(F32) * scales

    mine = lax.dynamic_slice_in_dim((scaled * gain).astype(BF16), core * half, half, 0)
    hidden_rows = hidden_in.astype(F32)
    inv = lax.rsqrt(jnp.mean(hidden_rows * hidden_rows, axis=1, keepdims=True) + 1e-05)
    cot_inv = (key_cotangent.astype(F32) * inv).astype(BF16)

    pieces = hidden_in.reshape(tok, nx, nh, nc, half).transpose(1, 3, 0, 2, 4)
    pieces = pieces.reshape(nx * nc, tok, nh * half)
    copies = jnp.broadcast_to(cot_inv[None], (nx * nc, tok, cols))
    sent, mine = lax.optimization_barrier((jnp.concatenate([pieces, copies], axis=2), mine))
    mate = lax.ppermute(mine, "yh", [(0, 1), (1, 0)])
    got = lax.all_to_all(sent, ("x", "c"), 0, 0)

    got, mate = lax.optimization_barrier((got, mate))
    low = lax.axis_index("yh") == 0
    pair = jnp.stack([jnp.where(low, mine, mate), jnp.where(low, mate, mine)])
    pair = pair.reshape(nh * half, cols)
    got, pair = lax.optimization_barrier((got, pair))
    own_half = lax.all_gather(pair, "x", axis=0, tiled=True)
    got = got.reshape(nx * nc * tok, nh * half + cols)
    product = lax.dot_general(
        got[:, : nh * half], got[:, nh * half :], (((0,), (0,)), ((), ())), preferred_element_type=F32
    ).astype(BF16)

    quarter = half // nl
    terms = lax.all_to_all(product.reshape(nh * nl, quarter, cols), ("yh", "yl"), 0, 0)
    summed = jnp.sum(terms.astype(F32), axis=0).astype(BF16)
    piece = -(-quarter // nz)
    summed = jnp.pad(summed, ((0, piece * nz - quarter), (0, 0))).reshape(nz, piece, cols)
    total = jnp.sum(lax.all_to_all(summed, "z", 0, 0).astype(F32), axis=0)
    scale = 1.0 / jnp.sqrt(F32(total_tokens))
    total = (total * scale).astype(BF16)

    whole = spread(total, "z", nz).reshape(nz * piece, cols)[:quarter]
    whole, own_half = lax.optimization_barrier((whole, own_half))
    other_half = lax.ppermute(own_half, "c", swap_c)
    whole = spread(whole, "yl", nl).reshape(half, cols)
    whole, other_half = lax.optimization_barrier((whole, other_half))
    whole = jnp.concatenate(by_core(whole, lax.ppermute(whole, "c", swap_c)), axis=0).astype(F32)
    weight_grad = (whole * gain).astype(BF16)
    gain_part = jnp.sum(whole * scaled.astype(BF16).astype(F32), axis=1)
    gain_gradient = spread(gain_part.reshape(-1, 128), ("x", "yh"), nx * nh).reshape(width)

    parts = by_core(own_half, other_half)
    gained = jnp.stack([p.reshape(nx * nh, half, cols) for p in parts], axis=1)
    gained = gained.reshape(width, cols)
    keys = jnp.dot(hidden_in, gained, preferred_element_type=F32) * inv
    keys_out = keys.astype(BF16)
    mean = jnp.sum(keys * key_cotangent.astype(F32), axis=1, keepdims=True) / width
    unit_gradient = lax.dot_general(
        key_cotangent, gained, (((1,), (1,)), ((), ())), preferred_element_type=F32
    )
    input_gradient = (inv * (unit_gradient - hidden_rows * inv * mean)).astype(BF16)
    return (keys_out, input_gradient, weight_grad, gain_gradient)


def solution(mesh):
    fine = Mesh(mesh.devices.reshape(4, 2, 4, 12, 2), ("x", "yh", "yl", "z", "c"))
    tokens = P(("x", "yh", "yl", "z", "c"), None)
    group = ("x", "yh")
    in_specs = (tokens, P(group), P(group, None), P(group, None), tokens)
    out_specs = (tokens, tokens, P(group, None), P())
    return jax.shard_map(body, mesh=fine, in_specs=in_specs, out_specs=out_specs, check_vma=False)
```

```python
import jax
import jax.numpy as jnp
from jax import lax
from jax.experimental import pallas as pl
from jax.experimental.pallas import tpu as pltpu
from jax.sharding import Mesh
from jax.sharding import PartitionSpec as P

F32 = jnp.float32
BF16 = jnp.bfloat16
VMEM = pl.BlockSpec(memory_space=pltpu.VMEM)
SMEM = pl.BlockSpec(memory_space=pltpu.SMEM)
PARAMS = pltpu.CompilerParams(vmem_limit_bytes=40 * 1024 * 1024)
SWAP = [(0, 1), (1, 0)]


def shape(dims, dtype):
    return jax.ShapeDtypeStruct(dims, dtype)


def prepare_kernel(hidden_ref, cot_ref, sent_ref, inv_ref):
    peers, tok, wide = sent_ref.shape
    cols = cot_ref.shape[1]
    part = wide - cols
    square = jnp.zeros((tok, 1), F32)
    for i in range(peers):
        piece = hidden_ref[:, i * part : (i + 1) * part]
        sent_ref[i, :, :part] = piece
        piece = piece.astype(F32)
        square = square + jnp.sum(piece * piece, axis=1, keepdims=True)
    inv = lax.rsqrt(square / (peers * part) + 1e-05)
    inv_ref[...] = inv
    scaled = (cot_ref[...].astype(F32) * inv).astype(BF16)
    for i in range(peers):
        sent_ref[i, :, part:] = scaled


def product_kernel(core_ref, got_ref, keep_ref, send_ref):
    peers, tok, wide = got_ref.shape
    groups, half, cols = keep_ref.shape
    part = wide - cols
    core = core_ref[0]
    cot = got_ref[:, :, part:].reshape(peers * tok, cols)
    for out_ref, which in ((send_ref, 1 - core), (keep_ref, core)):
        for g in range(groups):
            at = pl.multiple_of(g * 2 * half + which * half, half)
            left = got_ref[:, :, pl.ds(at, half)].reshape(peers * tok, half)
            value = lax.dot_general(left, cot, (((0,), (0,)), ((), ())), preferred_element_type=F32)
            out_ref[g] = value.astype(out_ref.dtype)


def finish_kernel(core_ref, own_ref, other_ref, weight_ref, gain_ref, grad_ref, part_ref):
    half = own_ref.shape[0]
    core = core_ref[0]
    for ref, which in ((own_ref, core), (other_ref, 1 - core)):
        rows = pl.ds(pl.multiple_of(which * half, half), half)
        value = ref[...].astype(F32)
        grad_ref[rows, :] = (value * gain_ref[rows, :]).astype(BF16)
        dots = jnp.sum(value * weight_ref[rows, :].astype(F32), axis=1, keepdims=True)
        part_ref[:, rows] = jnp.broadcast_to(dots, (half, 128)).T[:8]


def tokens_kernel(core_ref, hidden_ref, inv_ref, cot_ref, own_ref, other_ref, keys_ref, grad_ref):
    shifts, pairs, half, cols = own_ref.shape
    width = hidden_ref.shape[1]
    core, here = core_ref[0], core_ref[1]
    inv = inv_ref[...]
    cot = cot_ref[...]
    places = []
    for s in range(shifts):
        x = lax.rem(here - s + shifts, shifts)
        for g in range(pairs):
            for ref, which in ((own_ref, core), (other_ref, 1 - core)):
                at = pl.multiple_of(((x * pairs + g) * 2 + which) * half, half)
                places.append((ref.at[s, g], pl.ds(at, half)))
    keys = jnp.zeros(keys_ref.shape, F32)
    for ref, columns in places:
        keys = keys + jnp.dot(hidden_ref[:, columns], ref[...], preferred_element_type=F32)
    keys = keys * inv
    keys_ref[...] = keys.astype(BF16)
    mean = jnp.sum(keys * cot.astype(F32), axis=1, keepdims=True) / width
    for ref, columns in places:
        value = lax.dot_general(cot, ref[...], (((1,), (1,)), ((), ())), preferred_element_type=F32)
        unit = hidden_ref[:, columns].astype(F32) * inv
        grad_ref[:, columns] = (inv * (value - unit * mean)).astype(BF16)


def call(kernel, outs, specs, flops, moved):
    return pl.pallas_call(
        kernel,
        out_shape=outs,
        in_specs=specs,
        out_specs=jax.tree.map(lambda _: VMEM, outs),
        compiler_params=PARAMS,
        cost_estimate=pl.CostEstimate(flops=flops, bytes_accessed=moved, transcendentals=0),
    )


def spread(value, axes, size):
    copies = jnp.broadcast_to(value[None], (size,) + value.shape)
    return lax.all_to_all(copies, axes, 0, 0)


def tie(*values):
    return lax.optimization_barrier(values)


def body(hidden_in, norm_gain, key_codes, key_scales, key_cotangent):
    nx, nh, nl, nz, nc = (lax.axis_size(a) for a in ("x", "yh", "yl", "z", "c"))
    tok, width = hidden_in.shape
    rows, cols = key_codes.shape
    block = cols // key_scales.shape[1]
    total_tokens = tok * nx * nh * nl * nz * nc
    half = rows // nc
    core = lax.axis_index("c")
    core_at = jnp.stack([core, lax.axis_index("x")]).astype(jnp.int32)
    part = width // nx

    sent, inv = call(
        prepare_kernel,
        [shape((nx, tok, part + cols), BF16), shape((tok, 1), F32)],
        [VMEM, VMEM],
        4 * tok * width,
        4 * tok * width,
    )(hidden_in, key_cotangent)
    sent, key_codes = tie(sent, key_codes)
    got = lax.all_to_all(sent, "x", 0, 0)

    gain = norm_gain.astype(F32)[:, None]
    scales = jnp.repeat(key_scales.astype(F32), block, axis=1)
    scaled = key_codes.astype(F32) * scales
    weight = scaled.astype(BF16)
    mine = lax.dynamic_slice_in_dim((scaled * gain).astype(BF16), core * half, half, 0)
    mate = lax.ppermute(mine, "yh", SWAP)
    low = lax.axis_index("yh") == 0
    got, mine, mate, weight = tie(got, mine, mate, weight)

    keep, send = call(
        product_kernel,
        [shape((nh, half, cols), F32), shape((nh, half, cols), BF16)],
        [SMEM, VMEM],
        2 * nx * tok * part * cols,
        2 * nx * tok * (part + cols) + 6 * nh * half * cols,
    )(core_at, got)
    passed = lax.ppermute(send, "c", SWAP)
    pair = jnp.stack([jnp.where(low, mine, mate), jnp.where(low, mate, mine)])
    passed, pair = tie(passed, pair)
    product = (keep + passed.astype(F32)).astype(BF16)

    quarter = half // nl
    product, pair = tie(product.reshape(nh * nl, quarter, cols), pair)
    own = [pair]
    for s in range(1, nx):
        own.append(lax.ppermute(pair, "x", [(i, (i + s) % nx) for i in range(nx)]))
    terms = lax.all_to_all(product, ("yh", "yl"), 0, 0)
    summed = jnp.sum(terms.astype(F32), axis=0).astype(BF16)
    piece = -(-quarter // nz)
    summed = jnp.pad(summed, ((0, piece * nz - quarter), (0, 0))).reshape(nz, piece, cols)
    total = jnp.sum(lax.all_to_all(summed, "z", 0, 0).astype(F32), axis=0)
    scale = 1.0 / jnp.sqrt(F32(total_tokens))
    total = (total * scale).astype(BF16)

    whole = spread(total, "z", nz).reshape(nz * piece, cols)[:quarter]
    whole, *own = tie(whole, *own)
    own_half = jnp.stack(own)
    other_half = lax.ppermute(own_half, "c", SWAP)
    whole = spread(whole, "yl", nl).reshape(half, cols)
    passed = lax.ppermute(whole, "c", SWAP)
    weight_grad, gain_part = call(
        finish_kernel,
        [shape((rows, cols), BF16), shape((8, rows), F32)],
        [SMEM, VMEM, VMEM, VMEM, VMEM],
        4 * rows * cols,
        6 * rows * cols,
    )(core_at, whole, passed, weight, gain)
    gain_part, own_half, other_half = tie(gain_part[0].reshape(-1, 128), own_half, other_half)
    gain_gradient = spread(gain_part, ("x", "yh"), nx * nh).reshape(width)

    keys_out, input_gradient = call(
        tokens_kernel,
        [shape((tok, cols), BF16), shape((tok, width), BF16)],
        [SMEM, VMEM, VMEM, VMEM, VMEM, VMEM],
        4 * tok * width * cols,
        4 * tok * width + 2 * width * cols,
    )(core_at, hidden_in, inv, key_cotangent, own_half, other_half)
    return (keys_out, input_gradient, weight_grad, gain_gradient)


def solution(mesh):
    fine = Mesh(mesh.devices.reshape(4, 2, 4, 12, 2), ("x", "yh", "yl", "z", "c"))
    tokens = P(("x", "yh", "yl", "z", "c"), None)
    group = ("x", "yh")
    in_specs = (tokens, P(group), P(group, None), P(group, None), tokens)
    out_specs = (tokens, tokens, P(group, None), P())
    return jax.shard_map(body, mesh=fine, in_specs=in_specs, out_specs=out_specs, check_vma=False)
```

```python
import functools

import jax
import jax.numpy as jnp
from jax import lax
from jax.experimental import pallas as pl
from jax.experimental.pallas import tpu as pltpu
from jax.sharding import Mesh
from jax.sharding import PartitionSpec as P

F32 = jnp.float32
BF16 = jnp.bfloat16
VMEM = pl.BlockSpec(memory_space=pltpu.VMEM)
SMEM = pl.BlockSpec(memory_space=pltpu.SMEM)
HBM = pl.BlockSpec(memory_space=pltpu.HBM)
PARAMS = pltpu.CompilerParams(vmem_limit_bytes=12 * 1024 * 1024)
SWAP = [(0, 1), (1, 0)]
LANES = 128


def shape(dims, dtype):
    return jax.ShapeDtypeStruct(dims, dtype)


def down(row):
    return jnp.broadcast_to(row, (LANES, row.shape[1])).T


def gained_kernel(place_ref, codes_ref, scales_ref, gain_ref, out_ref):
    half, cols = out_ref.shape
    blocks = scales_ref.shape[0]
    rows = pl.ds(pl.multiple_of(place_ref[0] * half, half), half)
    gain = gain_ref[:, rows].astype(F32)
    for b in range(blocks):
        factor = down(scales_ref[b : b + 1, rows].astype(F32) * gain)
        for at in range(b * cols // blocks, (b + 1) * cols // blocks, LANES):
            columns = slice(at, at + LANES)
            out_ref[:, columns] = (codes_ref[rows, columns].astype(F32) * factor).astype(BF16)


def prepare_kernel(hidden_ref, cot_ref, sent_ref, hidden, cot, come, go):
    peers, tok, part = hidden.shape
    loads = [
        pltpu.make_async_copy(hidden_ref.at[:, pl.ds(i * part, part)], hidden.at[i], come.at[i]) for i in range(peers)
    ]
    loads.append(pltpu.make_async_copy(cot_ref, cot, come.at[peers]))
    for load in loads:
        load.start()
    stores = []
    square = jnp.zeros((tok, 1), F32)
    for i in range(peers):
        loads[i].wait()
        stores.append(pltpu.make_async_copy(hidden.at[i], sent_ref.at[i, :, pl.ds(0, part)], go.at[i]))
        stores[-1].start()
        piece = hidden[i].astype(F32)
        square = square + jnp.sum(piece * piece, axis=1, keepdims=True)
    inv = lax.rsqrt(square / (peers * part) + 1e-05)
    loads[peers].wait()
    cot[...] = (cot[...].astype(F32) * inv).astype(BF16)
    for i in range(peers):
        stores.append(pltpu.make_async_copy(cot, sent_ref.at[i, :, pl.ds(part, cot.shape[1])], go.at[peers + i]))
        stores[-1].start()
    for store in stores:
        store.wait()


def stack_kernel(*refs):
    for i, ref in enumerate(refs[:-1]):
        refs[-1][i] = ref[...]


def product_kernel(place_ref, got_ref, keep_ref, send_ref):
    peers, tok, wide = got_ref.shape
    groups, half, cols = keep_ref.shape
    part = wide - cols
    core = place_ref[0]
    cot = got_ref[:, :, part:].reshape(peers * tok, cols)
    for out_ref, which in ((send_ref, 1 - core), (keep_ref, core)):
        for g in range(groups):
            at = pl.multiple_of(g * 2 * half + which * half, half)
            left = got_ref[:, :, pl.ds(at, half)].reshape(peers * tok, half)
            value = lax.dot_general(left, cot, (((0,), (0,)), ((), ())), preferred_element_type=F32)
            out_ref[g] = value.astype(out_ref.dtype)


def finish_kernel(place_ref, total_ref, codes_ref, scales_ref, gain_ref, grad_ref, part_ref):
    half, cols = total_ref.shape
    blocks = scales_ref.shape[0]
    rows = pl.ds(pl.multiple_of(place_ref[0] * half, half), half)
    gain = down(gain_ref[:, rows].astype(F32))
    dots = jnp.zeros((half, LANES), F32)
    for b in range(blocks):
        scale = down(scales_ref[b : b + 1, rows].astype(F32))
        for at in range(b * cols // blocks, (b + 1) * cols // blocks, LANES):
            columns = slice(at, at + LANES)
            value = total_ref[:, columns].astype(F32)
            weight = (codes_ref[rows, columns].astype(F32) * scale).astype(BF16)
            dots = dots + value * weight.astype(F32)
            grad_ref[:, columns] = (value * gain).astype(BF16)
    for i in range(half // LANES):
        row = jnp.sum(dots[i * LANES : (i + 1) * LANES].T, axis=0, keepdims=True)
        for peer in range(part_ref.shape[0]):
            part_ref[peer, i : i + 1, :] = row


def tokens_kernel(place_ref, hidden_ref, cot_ref, own_ref, other_ref, keys_ref, grad_ref):
    shifts, pairs, half, cols = own_ref.shape
    width = hidden_ref.shape[1]
    core, here, side = place_ref[0], place_ref[1], place_ref[2]
    square = jnp.zeros((hidden_ref.shape[0], 1), F32)
    for at in range(0, width, width // 4):
        piece = hidden_ref[:, at : at + width // 4].astype(F32)
        square = square + jnp.sum(piece * piece, axis=1, keepdims=True)
    inv = lax.rsqrt(square / width + 1e-05)
    cot = cot_ref[...]
    places = []
    for s in range(shifts):
        x = lax.rem(here - s + shifts, shifts)
        for j in range(pairs):
            y = lax.rem(side + j, pairs)
            for ref, which in ((own_ref, core), (other_ref, 1 - core)):
                at = pl.multiple_of(((x * pairs + y) * 2 + which) * half, half)
                places.append((ref.at[s, j], pl.ds(at, half)))
    keys = jnp.zeros(keys_ref.shape, F32)
    for ref, columns in places:
        keys = keys + jnp.dot(hidden_ref[:, columns], ref[...], preferred_element_type=F32)
    keys = keys * inv
    keys_ref[...] = keys.astype(BF16)
    mean = jnp.sum(keys * cot.astype(F32), axis=1, keepdims=True) / width
    for ref, columns in places:
        value = lax.dot_general(cot, ref[...], (((1,), (1,)), ((), ())), preferred_element_type=F32)
        unit = hidden_ref[:, columns].astype(F32) * inv
        grad_ref[:, columns] = (inv * (value - unit * mean)).astype(BF16)


def halve_kernel(place_ref, terms_ref, keep_ref, send_ref):
    rows = keep_ref.shape[0]
    mine = place_ref[3]
    for ref, which in ((send_ref, 1 - mine), (keep_ref, mine)):
        at = pl.ds(pl.multiple_of(which * rows, rows), rows)
        total = terms_ref[0, at, :].astype(F32)
        for i in range(1, terms_ref.shape[0]):
            total = total + terms_ref[i, at, :].astype(F32)
        ref[...] = total.astype(BF16)


def add_kernel(keep_ref, came_ref, copies_ref):
    total = (keep_ref[...].astype(F32) + came_ref[...].astype(F32)).astype(BF16)
    for i in range(copies_ref.shape[0]):
        copies_ref[i] = total


def total_kernel(scale, terms_ref, copies_ref):
    total = terms_ref[0].astype(F32)
    for i in range(1, terms_ref.shape[0]):
        total = total + terms_ref[i].astype(F32)
    total = (total * scale).astype(BF16)
    for i in range(copies_ref.shape[0]):
        copies_ref[i] = total


def gains_kernel(place_ref, own_ref, other_ref, out_ref):
    groups, deep, _ = own_ref.shape
    core = place_ref[0]
    for g in range(groups):
        for ref, which in ((own_ref, core), (other_ref, 1 - core)):
            out_ref[pl.ds((g * 2 + which) * deep, deep), :] = ref[g]


def call(kernel, outs, specs, flops, moved, after=()):
    count = len(specs)

    def run(*refs):
        kernel(*refs[:count], *refs[count + len(after) :])

    made = pl.pallas_call(
        run,
        out_shape=outs,
        in_specs=specs + [pl.BlockSpec(memory_space=pl.ANY)] * len(after),
        out_specs=jax.tree.map(lambda _: VMEM, outs),
        compiler_params=PARAMS,
        cost_estimate=pl.CostEstimate(flops=flops, bytes_accessed=moved, transcendentals=0),
    )
    return lambda *operands: made(*operands, *after)


def tie(*values):
    return lax.optimization_barrier(values)


def by_core(own, other):
    first = lax.axis_index("c") == 0
    return jnp.where(first, own, other), jnp.where(first, other, own)


def body(hidden_in, norm_gain, key_codes, key_scales, key_cotangent):
    nx, nh, nl, nz, np, nc = (lax.axis_size(a) for a in ("x", "yh", "yl", "z", "zp", "c"))
    tok, width = hidden_in.shape
    rows, cols = key_codes.shape
    total_tokens = tok * nx * nh * nl * nz * np * nc
    half = rows // nc
    part = width // nx
    place = jnp.stack([lax.axis_index(a) for a in ("c", "x", "yh", "zp")]).astype(jnp.int32)
    scales, gain = key_scales.T, norm_gain[None]

    sent = pl.pallas_call(
        prepare_kernel,
        out_shape=shape((nx, tok, part + cols), BF16),
        in_specs=[HBM] * 2,
        out_specs=HBM,
        scratch_shapes=[
            pltpu.VMEM((nx, tok, part), BF16),
            pltpu.VMEM((tok, cols), BF16),
            pltpu.SemaphoreType.DMA((nx + 1,)),
            pltpu.SemaphoreType.DMA((2 * nx,)),
        ],
        compiler_params=PARAMS,
        cost_estimate=pl.CostEstimate(flops=4 * tok * width, bytes_accessed=4 * tok * width, transcendentals=0),
    )(hidden_in, key_cotangent)
    got = lax.all_to_all(sent, "x", 0, 0)

    mine = call(gained_kernel, shape((half, cols), BF16), [SMEM, VMEM, VMEM, VMEM], half * cols, 4 * half * cols, [sent])(
        place, key_codes, scales, gain
    )
    mate = lax.ppermute(mine, "yh", SWAP)

    keep, send = call(
        product_kernel,
        [shape((nh, half, cols), F32), shape((nh, half, cols), BF16)],
        [SMEM, VMEM],
        2 * nx * tok * part * cols,
        2 * nx * tok * (part + cols) + 6 * nh * half * cols,
        [mate],
    )(place, got)
    product = (keep + lax.ppermute(send, "c", SWAP).astype(F32)).astype(BF16)
    pair = call(stack_kernel, shape((nh, half, cols), BF16), [VMEM] * 2, 0, 4 * nh * half * cols, [product])(mine, mate)

    quarter = half // nl
    eighth = quarter // np
    own = [pair] + [lax.ppermute(pair, "x", [(i, (i + s) % nx) for i in range(nx)]) for s in range(1, nx)]
    terms = lax.all_to_all(product.reshape(nh * nl, quarter, cols), ("yh", "yl"), 0, 0)
    keep, send = call(
        halve_kernel, [shape((eighth, cols), BF16)] * 2, [SMEM, VMEM], nh * nl * quarter * cols, 2 * half * cols
    )(place, terms)
    copies = call(
        add_kernel, shape((nz, eighth, cols), BF16), [VMEM, VMEM], eighth * cols, 2 * nz * eighth * cols
    )(keep, lax.ppermute(send, "zp", SWAP))
    own = call(stack_kernel, shape((nx, nh, half, cols), BF16), [VMEM] * nx, 0, 4 * width * cols, [keep])(*own)
    other = lax.ppermute(own, "c", SWAP)
    scale = float(total_tokens) ** -0.5
    copies = call(
        functools.partial(total_kernel, scale),
        shape((nl * np, eighth, cols), BF16),
        [VMEM],
        nz * eighth * cols,
        2 * (nz + nl * np) * eighth * cols,
        [other],
    )(lax.all_to_all(copies, "z", 0, 0))

    whole = lax.all_to_all(copies, ("yl", "zp"), 0, 0).reshape(half, cols)
    keys_out, input_gradient = call(
        tokens_kernel,
        [shape((tok, cols), BF16), shape((tok, width), BF16)],
        [SMEM, VMEM, VMEM, VMEM, VMEM],
        4 * tok * width * cols,
        4 * tok * width + 2 * width * cols,
    )(place, hidden_in, key_cotangent, own, other)
    whole, keys_out = tie(whole, keys_out)
    grad_half, gain_half = call(
        finish_kernel,
        [shape((half, cols), BF16), shape((nx * nh, half // LANES, LANES), F32)],
        [SMEM, VMEM, VMEM, VMEM, VMEM],
        4 * half * cols,
        6 * half * cols,
    )(place, whole, key_codes, scales, gain)
    gains = lax.all_to_all(gain_half, ("x", "yh"), 0, 0)
    weight_grad = jnp.concatenate(by_core(grad_half, lax.ppermute(grad_half, "c", SWAP)), axis=0)
    gains, weight_grad = tie(gains, weight_grad)
    gain_gradient = call(
        gains_kernel, shape((width // LANES, LANES), F32), [SMEM, VMEM, VMEM], width, 8 * width
    )(place, gains, lax.ppermute(gains, "c", SWAP)).reshape(width)
    return (keys_out, input_gradient, weight_grad, gain_gradient)


def solution(mesh):
    axes = ("x", "yh", "yl", "z", "zp", "c")
    fine = Mesh(mesh.devices.reshape(4, 2, 4, 6, 2, 2), axes)
    tokens = P(axes, None)
    group = ("x", "yh")
    in_specs = (tokens, P(group), P(group, None), P(group, None), tokens)
    out_specs = (tokens, tokens, P(group, None), P())
    return jax.shard_map(body, mesh=fine, in_specs=in_specs, out_specs=out_specs, check_vma=False)
```

```python
import functools

import jax
import jax.numpy as jnp
from jax import lax
from jax.experimental import pallas as pl
from jax.experimental.pallas import tpu as pltpu
from jax.sharding import Mesh
from jax.sharding import PartitionSpec as P

F32 = jnp.float32
BF16 = jnp.bfloat16
VMEM = pl.BlockSpec(memory_space=pltpu.VMEM)
SMEM = pl.BlockSpec(memory_space=pltpu.SMEM)
HBM = pl.BlockSpec(memory_space=pltpu.HBM)
PARAMS = pltpu.CompilerParams(vmem_limit_bytes=12 * 1024 * 1024)
SWAP = [(0, 1), (1, 0)]
LANES = 128


def shape(dims, dtype):
    return jax.ShapeDtypeStruct(dims, dtype)


def down(row):
    return jnp.broadcast_to(row, (LANES, row.shape[1])).T


def gained_kernel(place_ref, codes_ref, scales_ref, gain_ref, out_ref):
    half, cols = out_ref.shape
    blocks = scales_ref.shape[0]
    rows = pl.ds(pl.multiple_of(place_ref[0] * half, half), half)
    gain = gain_ref[:, rows].astype(F32)
    for b in range(blocks):
        factor = down(scales_ref[b : b + 1, rows].astype(F32) * gain)
        for at in range(b * cols // blocks, (b + 1) * cols // blocks, LANES):
            columns = slice(at, at + LANES)
            out_ref[:, columns] = (codes_ref[rows, columns].astype(F32) * factor).astype(BF16)


def prepare_kernel(hidden_ref, cot_ref, sent_ref, mark_ref, hidden, cot, come, go):
    peers, tok, part = hidden.shape
    loads = [
        pltpu.make_async_copy(hidden_ref.at[:, pl.ds(i * part, part)], hidden.at[i], come.at[i]) for i in range(peers)
    ]
    loads.append(pltpu.make_async_copy(cot_ref, cot, come.at[peers]))
    for load in loads:
        load.start()
    stores = []
    square = jnp.zeros((tok, 1), F32)
    for i in range(peers):
        loads[i].wait()
        stores.append(pltpu.make_async_copy(hidden.at[i], sent_ref.at[i, :, pl.ds(0, part)], go.at[i]))
        stores[-1].start()
        piece = hidden[i].astype(F32)
        square = square + jnp.sum(piece * piece, axis=1, keepdims=True)
    inv = lax.rsqrt(square / (peers * part) + 1e-05)
    loads[peers].wait()
    cot[...] = (cot[...].astype(F32) * inv).astype(BF16)
    for i in range(peers):
        stores.append(pltpu.make_async_copy(cot, sent_ref.at[i, :, pl.ds(part, cot.shape[1])], go.at[peers + i]))
        stores[-1].start()
    mark_ref[...] = square[:8]
    for store in stores:
        store.wait()


def stack_kernel(*refs):
    for i, ref in enumerate(refs[:-1]):
        refs[-1][i] = ref[...]


def product_kernel(place_ref, got_ref, keep_ref, send_ref):
    peers, tok, wide = got_ref.shape
    groups, half, cols = keep_ref.shape
    part = wide - cols
    core = place_ref[0]
    cot = got_ref[:, :, part:].reshape(peers * tok, cols)
    for out_ref, which in ((send_ref, 1 - core), (keep_ref, core)):
        for g in range(groups):
            at = pl.multiple_of(g * 2 * half + which * half, half)
            left = got_ref[:, :, pl.ds(at, half)].reshape(peers * tok, half)
            value = lax.dot_general(left, cot, (((0,), (0,)), ((), ())), preferred_element_type=F32)
            out_ref[g] = value.astype(out_ref.dtype)


def dots_kernel(place_ref, total_ref, codes_ref, scales_ref, part_ref):
    half, cols = total_ref.shape
    blocks = scales_ref.shape[0]
    rows = pl.ds(pl.multiple_of(place_ref[0] * half, half), half)
    dots = jnp.zeros((half, LANES), F32)
    for b in range(blocks):
        scale = down(scales_ref[b : b + 1, rows].astype(F32))
        for at in range(b * cols // blocks, (b + 1) * cols // blocks, LANES):
            columns = slice(at, at + LANES)
            weight = (codes_ref[rows, columns].astype(F32) * scale).astype(BF16)
            dots = dots + total_ref[:, columns].astype(F32) * weight.astype(F32)
    for i in range(half // LANES):
        row = jnp.sum(dots[i * LANES : (i + 1) * LANES].T, axis=0, keepdims=True)
        for peer in range(part_ref.shape[0]):
            part_ref[peer, i : i + 1, :] = row


def finish_kernel(place_ref, total_ref, gain_ref, grad_ref):
    half, cols = total_ref.shape
    rows = pl.ds(pl.multiple_of(place_ref[0] * half, half), half)
    gain = down(gain_ref[:, rows].astype(F32))
    for at in range(0, cols, LANES):
        columns = slice(at, at + LANES)
        grad_ref[:, columns] = (total_ref[:, columns].astype(F32) * gain).astype(BF16)


def tokens_kernel(place_ref, hidden_ref, cot_ref, own_ref, other_ref, keys_ref, grad_ref):
    shifts, pairs, half, cols = own_ref.shape
    width = hidden_ref.shape[1]
    core, here, side = place_ref[0], place_ref[1], place_ref[2]
    square = jnp.zeros((hidden_ref.shape[0], 1), F32)
    for at in range(0, width, width // 4):
        piece = hidden_ref[:, at : at + width // 4].astype(F32)
        square = square + jnp.sum(piece * piece, axis=1, keepdims=True)
    inv = lax.rsqrt(square / width + 1e-05)
    cot = cot_ref[...]
    places = []
    for s in range(shifts):
        x = lax.rem(here - s + shifts, shifts)
        for j in range(pairs):
            y = lax.rem(side + j, pairs)
            for ref, which in ((own_ref, core), (other_ref, 1 - core)):
                at = pl.multiple_of(((x * pairs + y) * 2 + which) * half, half)
                places.append((ref.at[s, j], pl.ds(at, half)))
    keys = jnp.zeros(keys_ref.shape, F32)
    for ref, columns in places:
        keys = keys + jnp.dot(hidden_ref[:, columns], ref[...], preferred_element_type=F32)
    keys = keys * inv
    keys_ref[...] = keys.astype(BF16)
    mean = jnp.sum(keys * cot.astype(F32), axis=1, keepdims=True) / width
    for ref, columns in places:
        value = lax.dot_general(cot, ref[...], (((1,), (1,)), ((), ())), preferred_element_type=F32)
        unit = hidden_ref[:, columns].astype(F32) * inv
        grad_ref[:, columns] = (inv * (value - unit * mean)).astype(BF16)


def halve_kernel(place_ref, terms_ref, keep_ref, send_ref):
    rows = keep_ref.shape[0]
    mine = place_ref[3]
    for ref, which in ((send_ref, 1 - mine), (keep_ref, mine)):
        at = pl.ds(pl.multiple_of(which * rows, rows), rows)
        total = terms_ref[0, at, :].astype(F32)
        for i in range(1, terms_ref.shape[0]):
            total = total + terms_ref[i, at, :].astype(F32)
        ref[...] = total.astype(BF16)


def add_kernel(keep_ref, came_ref, copies_ref):
    total = (keep_ref[...].astype(F32) + came_ref[...].astype(F32)).astype(BF16)
    for i in range(copies_ref.shape[0]):
        copies_ref[i] = total


def total_kernel(scale, terms_ref, copies_ref):
    total = terms_ref[0].astype(F32)
    for i in range(1, terms_ref.shape[0]):
        total = total + terms_ref[i].astype(F32)
    total = (total * scale).astype(BF16)
    for i in range(copies_ref.shape[0]):
        copies_ref[i] = total


def gains_kernel(place_ref, own_ref, other_ref, out_ref):
    groups, deep, _ = own_ref.shape
    core = place_ref[0]
    for g in range(groups):
        for ref, which in ((own_ref, core), (other_ref, 1 - core)):
            out_ref[pl.ds((g * 2 + which) * deep, deep), :] = ref[g]


def call(kernel, outs, specs, flops, moved, after=()):
    count = len(specs)

    def run(*refs):
        kernel(*refs[:count], *refs[count + len(after) :])

    made = pl.pallas_call(
        run,
        out_shape=outs,
        in_specs=specs + [pl.BlockSpec(memory_space=pl.ANY)] * len(after),
        out_specs=jax.tree.map(lambda _: VMEM, outs),
        compiler_params=PARAMS,
        cost_estimate=pl.CostEstimate(flops=flops, bytes_accessed=moved, transcendentals=0),
    )
    return lambda *operands: made(*operands, *after)


def tie(*values):
    return lax.optimization_barrier(values)


def by_core(own, other):
    first = lax.axis_index("c") == 0
    return jnp.where(first, own, other), jnp.where(first, other, own)


def body(hidden_in, norm_gain, key_codes, key_scales, key_cotangent):
    nx, nh, nl, nz, np, nc = (lax.axis_size(a) for a in ("x", "yh", "yl", "z", "zp", "c"))
    tok, width = hidden_in.shape
    rows, cols = key_codes.shape
    total_tokens = tok * nx * nh * nl * nz * np * nc
    half = rows // nc
    part = width // nx
    place = jnp.stack([lax.axis_index(a) for a in ("c", "x", "yh", "zp")]).astype(jnp.int32)
    scales, gain = key_scales.T, norm_gain[None]

    sent, mark = pl.pallas_call(
        prepare_kernel,
        out_shape=[shape((nx, tok, part + cols), BF16), shape((8, 1), F32)],
        in_specs=[HBM] * 2,
        out_specs=[HBM, VMEM],
        scratch_shapes=[
            pltpu.VMEM((nx, tok, part), BF16),
            pltpu.VMEM((tok, cols), BF16),
            pltpu.SemaphoreType.DMA((nx + 1,)),
            pltpu.SemaphoreType.DMA((2 * nx,)),
        ],
        compiler_params=pltpu.CompilerParams(vmem_limit_bytes=60 * 1024 * 1024),
        cost_estimate=pl.CostEstimate(flops=4 * tok * width, bytes_accessed=4 * tok * width, transcendentals=0),
    )(hidden_in, key_cotangent)
    got = lax.all_to_all(sent, "x", 0, 0)

    mine = call(gained_kernel, shape((half, cols), BF16), [SMEM, VMEM, VMEM, VMEM], half * cols, 4 * half * cols, [mark])(
        place, key_codes, scales, gain
    )
    mate = lax.ppermute(mine, "yh", SWAP)

    keep, send = call(
        product_kernel,
        [shape((nh, half, cols), F32), shape((nh, half, cols), BF16)],
        [SMEM, VMEM],
        2 * nx * tok * part * cols,
        2 * nx * tok * (part + cols) + 6 * nh * half * cols,
        [mate],
    )(place, got)
    product = (keep + lax.ppermute(send, "c", SWAP).astype(F32)).astype(BF16)
    pair = call(stack_kernel, shape((nh, half, cols), BF16), [VMEM] * 2, 0, 4 * nh * half * cols, [product])(mine, mate)

    quarter = half // nl
    eighth = quarter // np
    own = [pair] + [lax.ppermute(pair, "x", [(i, (i + s) % nx) for i in range(nx)]) for s in range(1, nx)]
    terms = lax.all_to_all(product.reshape(nh * nl, quarter, cols), ("yh", "yl"), 0, 0)
    keep, send = call(
        halve_kernel, [shape((eighth, cols), BF16)] * 2, [SMEM, VMEM], nh * nl * quarter * cols, 2 * half * cols, [own[1], own[-1]]
    )(place, terms)
    copies = call(
        add_kernel, shape((nz, eighth, cols), BF16), [VMEM, VMEM], eighth * cols, 2 * nz * eighth * cols
    )(keep, lax.ppermute(send, "zp", SWAP))
    scale = float(total_tokens) ** -0.5
    terms = lax.all_to_all(copies, "z", 0, 0)
    copies = call(
        functools.partial(total_kernel, scale),
        shape((nl * np, eighth, cols), BF16),
        [VMEM],
        nz * eighth * cols,
        2 * (nz + nl * np) * eighth * cols,
    )(terms)

    whole = lax.all_to_all(copies, ("yl", "zp"), 0, 0).reshape(half, cols)
    own = call(stack_kernel, shape((nx, nh, half, cols), BF16), [VMEM] * nx, 0, 4 * width * cols, [copies])(*own)
    other = lax.ppermute(own, "c", SWAP)
    gain_half = call(
        dots_kernel,
        shape((nx * nh, half // LANES, LANES), F32),
        [SMEM, VMEM, VMEM, VMEM],
        2 * half * cols,
        4 * half * cols,
    )(place, whole, key_codes, scales)
    grad_half = call(
        finish_kernel, shape((half, cols), BF16), [SMEM, VMEM, VMEM], half * cols, 4 * half * cols, [gain_half]
    )(place, whole, gain)
    keys_out, input_gradient = call(
        tokens_kernel,
        [shape((tok, cols), BF16), shape((tok, width), BF16)],
        [SMEM, VMEM, VMEM, VMEM, VMEM],
        4 * tok * width * cols,
        4 * tok * width + 2 * width * cols,
        [grad_half],
    )(place, hidden_in, key_cotangent, own, other)
    gains = lax.all_to_all(gain_half, ("x", "yh"), 0, 0)
    weight_grad = jnp.concatenate(by_core(grad_half, lax.ppermute(grad_half, "c", SWAP)), axis=0)
    gains, keys_out = tie(gains, keys_out)
    gain_gradient = call(
        gains_kernel, shape((width // LANES, LANES), F32), [SMEM, VMEM, VMEM], width, 8 * width
    )(place, gains, lax.ppermute(gains, "c", SWAP)).reshape(width)
    return (keys_out, input_gradient, weight_grad, gain_gradient)


def solution(mesh):
    axes = ("x", "yh", "yl", "z", "zp", "c")
    fine = Mesh(mesh.devices.reshape(4, 2, 4, 6, 2, 2), axes)
    tokens = P(axes, None)
    group = ("x", "yh")
    in_specs = (tokens, P(group), P(group, None), P(group, None), tokens)
    out_specs = (tokens, tokens, P(group, None), P())
    return jax.shard_map(body, mesh=fine, in_specs=in_specs, out_specs=out_specs, check_vma=False)
```

```python
import functools

import jax
import jax.numpy as jnp
from jax import lax
from jax.experimental import pallas as pl
from jax.experimental.pallas import tpu as pltpu
from jax.sharding import Mesh
from jax.sharding import PartitionSpec as P

F32 = jnp.float32
BF16 = jnp.bfloat16
VMEM = pl.BlockSpec(memory_space=pltpu.VMEM)
SMEM = pl.BlockSpec(memory_space=pltpu.SMEM)
HBM = pl.BlockSpec(memory_space=pltpu.HBM)
PARAMS = pltpu.CompilerParams(vmem_limit_bytes=12 * 1024 * 1024)
SWAP = [(0, 1), (1, 0)]
LANES = 128


def shape(dims, dtype):
    return jax.ShapeDtypeStruct(dims, dtype)


def down(row):
    return jnp.broadcast_to(row, (LANES, row.shape[1])).T


def gained_kernel(place_ref, codes_ref, scales_ref, gain_ref, out_ref):
    half, cols = out_ref.shape
    blocks = scales_ref.shape[0]
    rows = pl.ds(pl.multiple_of(place_ref[0] * half, half), half)
    gain = gain_ref[:, rows].astype(F32)
    for b in range(blocks):
        factor = down(scales_ref[b : b + 1, rows].astype(F32) * gain)
        for at in range(b * cols // blocks, (b + 1) * cols // blocks, LANES):
            columns = slice(at, at + LANES)
            out_ref[:, columns] = (codes_ref[rows, columns].astype(F32) * factor).astype(BF16)


def prepare_kernel(hidden_ref, cot_ref, sent_ref, mark_ref, hidden, cot, come, go):
    peers, tok, part = hidden.shape
    loads = [
        pltpu.make_async_copy(hidden_ref.at[:, pl.ds(i * part, part)], hidden.at[i], come.at[i]) for i in range(peers)
    ]
    loads.append(pltpu.make_async_copy(cot_ref, cot, come.at[peers]))
    for load in loads:
        load.start()
    stores = []
    square = jnp.zeros((tok, 1), F32)
    for i in range(peers):
        loads[i].wait()
        stores.append(pltpu.make_async_copy(hidden.at[i], sent_ref.at[i, :, pl.ds(0, part)], go.at[i]))
        stores[-1].start()
        piece = hidden[i].astype(F32)
        square = square + jnp.sum(piece * piece, axis=1, keepdims=True)
    inv = lax.rsqrt(square / (peers * part) + 1e-05)
    loads[peers].wait()
    cot[...] = (cot[...].astype(F32) * inv).astype(BF16)
    for i in range(peers):
        stores.append(pltpu.make_async_copy(cot, sent_ref.at[i, :, pl.ds(part, cot.shape[1])], go.at[peers + i]))
        stores[-1].start()
    mark_ref[...] = square[:8]
    for store in stores:
        store.wait()


def stack_kernel(*refs):
    for i, ref in enumerate(refs[:-1]):
        refs[-1][i] = ref[...]


def product_kernel(place_ref, got_ref, keep_ref, send_ref):
    peers, tok, wide = got_ref.shape
    groups, half, cols = keep_ref.shape
    part = wide - cols
    core = place_ref[0]
    cot = got_ref[:, :, part:].reshape(peers * tok, cols)
    for out_ref, which in ((send_ref, 1 - core), (keep_ref, core)):
        for g in range(groups):
            at = pl.multiple_of(g * 2 * half + which * half, half)
            left = got_ref[:, :, pl.ds(at, half)].reshape(peers * tok, half)
            value = lax.dot_general(left, cot, (((0,), (0,)), ((), ())), preferred_element_type=F32)
            out_ref[g] = value.astype(out_ref.dtype)


def marked_stack_kernel(*refs):
    stack_kernel(*refs[:-1])
    refs[-1][...] = refs[0][0, :16, :LANES]


def row_dots(at, total_ref, codes_ref, scales_ref):
    half, cols = total_ref.shape
    blocks = scales_ref.shape[0]
    rows = pl.ds(pl.multiple_of(at, half), half)
    dots = jnp.zeros((half, LANES), F32)
    for b in range(blocks):
        scale = down(scales_ref[b : b + 1, rows].astype(F32))
        for c in range(b * cols // blocks, (b + 1) * cols // blocks, LANES):
            columns = slice(c, c + LANES)
            weight = (codes_ref[rows, columns].astype(F32) * scale).astype(BF16)
            dots = dots + total_ref[:, columns].astype(F32) * weight.astype(F32)
    parts = [dots[i : i + LANES].T for i in range(0, half, LANES)]
    return [jnp.sum(part, axis=0, keepdims=True) for part in parts]


def dots_kernel(place_ref, total_ref, codes_ref, scales_ref, part_ref):
    for i, row in enumerate(row_dots(place_ref[0] * total_ref.shape[0], total_ref, codes_ref, scales_ref)):
        part_ref[i : i + 1, :] = row


def pair_dots_kernel(place_ref, own_ref, total_ref, codes_ref, scales_ref, part_ref):
    core = place_ref[0]
    deep = own_ref.shape[0]
    found = row_dots((1 - core) * total_ref.shape[0], total_ref, codes_ref, scales_ref)
    for peer in range(part_ref.shape[0]):
        part_ref[peer, pl.ds(core * deep, deep), :] = own_ref[...]
        for i, row in enumerate(found):
            part_ref[peer, pl.ds((1 - core) * deep + i, 1), :] = row


def finish_kernel(place_ref, own_ref, other_ref, gain_ref, grad_ref):
    half, cols = own_ref.shape
    core = place_ref[0]
    for ref, which in ((own_ref, core), (other_ref, 1 - core)):
        rows = pl.ds(pl.multiple_of(which * half, half), half)
        gain = down(gain_ref[:, rows].astype(F32))
        for at in range(0, cols, LANES):
            columns = slice(at, at + LANES)
            grad_ref[rows, columns] = (ref[:, columns].astype(F32) * gain).astype(BF16)


def tokens_kernel(place_ref, hidden_ref, cot_ref, own_ref, other_ref, keys_ref, grad_ref):
    shifts, pairs, half, cols = own_ref.shape
    width = hidden_ref.shape[1]
    core, here, side = place_ref[0], place_ref[1], place_ref[2]
    square = jnp.zeros((hidden_ref.shape[0], 1), F32)
    for at in range(0, width, width // 4):
        piece = hidden_ref[:, at : at + width // 4].astype(F32)
        square = square + jnp.sum(piece * piece, axis=1, keepdims=True)
    inv = lax.rsqrt(square / width + 1e-05)
    cot = cot_ref[...]
    places = []
    for s in range(shifts):
        x = lax.rem(here - s + shifts, shifts)
        for j in range(pairs):
            y = lax.rem(side + j, pairs)
            for ref, which in ((own_ref, core), (other_ref, 1 - core)):
                at = pl.multiple_of(((x * pairs + y) * 2 + which) * half, half)
                places.append((ref.at[s, j], pl.ds(at, half)))
    keys = jnp.zeros(keys_ref.shape, F32)
    for ref, columns in places:
        keys = keys + jnp.dot(hidden_ref[:, columns], ref[...], preferred_element_type=F32)
    keys = keys * inv
    keys_ref[...] = keys.astype(BF16)
    mean = jnp.sum(keys * cot.astype(F32), axis=1, keepdims=True) / width
    for ref, columns in places:
        value = lax.dot_general(cot, ref[...], (((1,), (1,)), ((), ())), preferred_element_type=F32)
        unit = hidden_ref[:, columns].astype(F32) * inv
        grad_ref[:, columns] = (inv * (value - unit * mean)).astype(BF16)


def halve_kernel(place_ref, terms_ref, keep_ref, send_ref):
    rows = keep_ref.shape[0]
    mine = place_ref[3]
    for ref, which in ((send_ref, 1 - mine), (keep_ref, mine)):
        at = pl.ds(pl.multiple_of(which * rows, rows), rows)
        total = terms_ref[0, at, :].astype(F32)
        for i in range(1, terms_ref.shape[0]):
            total = total + terms_ref[i, at, :].astype(F32)
        ref[...] = total.astype(BF16)


def add_kernel(keep_ref, came_ref, copies_ref):
    total = (keep_ref[...].astype(F32) + came_ref[...].astype(F32)).astype(BF16)
    for i in range(copies_ref.shape[0]):
        copies_ref[i] = total


def total_kernel(scale, terms_ref, copies_ref):
    total = terms_ref[0].astype(F32)
    for i in range(1, terms_ref.shape[0]):
        total = total + terms_ref[i].astype(F32)
    total = (total * scale).astype(BF16)
    for i in range(copies_ref.shape[0]):
        copies_ref[i] = total


def call(kernel, outs, specs, flops, moved, after=()):
    count = len(specs)

    def run(*refs):
        kernel(*refs[:count], *refs[count + len(after) :])

    made = pl.pallas_call(
        run,
        out_shape=outs,
        in_specs=specs + [pl.BlockSpec(memory_space=pl.ANY)] * len(after),
        out_specs=jax.tree.map(lambda _: VMEM, outs),
        compiler_params=PARAMS,
        cost_estimate=pl.CostEstimate(flops=flops, bytes_accessed=moved, transcendentals=0),
    )
    return lambda *operands: made(*operands, *after)


def tie(*values):
    return lax.optimization_barrier(values)


def body(hidden_in, norm_gain, key_codes, key_scales, key_cotangent):
    nx, nh, nl, nz, np, nc = (lax.axis_size(a) for a in ("x", "yh", "yl", "z", "zp", "c"))
    tok, width = hidden_in.shape
    rows, cols = key_codes.shape
    total_tokens = tok * nx * nh * nl * nz * np * nc
    half = rows // nc
    part = width // nx
    place = jnp.stack([lax.axis_index(a) for a in ("c", "x", "yh", "zp")]).astype(jnp.int32)
    scales, gain = key_scales.T, norm_gain[None]

    sent, mark = pl.pallas_call(
        prepare_kernel,
        out_shape=[shape((nx, tok, part + cols), BF16), shape((8, 1), F32)],
        in_specs=[HBM] * 2,
        out_specs=[HBM, VMEM],
        scratch_shapes=[
            pltpu.VMEM((nx, tok, part), BF16),
            pltpu.VMEM((tok, cols), BF16),
            pltpu.SemaphoreType.DMA((nx + 1,)),
            pltpu.SemaphoreType.DMA((2 * nx,)),
        ],
        compiler_params=pltpu.CompilerParams(vmem_limit_bytes=60 * 1024 * 1024),
        cost_estimate=pl.CostEstimate(flops=4 * tok * width, bytes_accessed=4 * tok * width, transcendentals=0),
    )(hidden_in, key_cotangent)
    got = lax.all_to_all(sent, "x", 0, 0)

    mine = call(gained_kernel, shape((half, cols), BF16), [SMEM, VMEM, VMEM, VMEM], half * cols, 4 * half * cols, [mark])(
        place, key_codes, scales, gain
    )
    mate = lax.ppermute(mine, "yh", SWAP)

    keep, send = call(
        product_kernel,
        [shape((nh, half, cols), F32), shape((nh, half, cols), BF16)],
        [SMEM, VMEM],
        2 * nx * tok * part * cols,
        2 * nx * tok * (part + cols) + 6 * nh * half * cols,
        [mate],
    )(place, got)
    product = (keep + lax.ppermute(send, "c", SWAP).astype(F32)).astype(BF16)
    pair = call(stack_kernel, shape((nh, half, cols), BF16), [VMEM] * 2, 0, 4 * nh * half * cols, [product])(mine, mate)

    quarter = half // nl
    eighth = quarter // np
    own = [pair] + [lax.ppermute(pair, "x", [(i, (i + s) % nx) for i in range(nx)]) for s in range(1, nx)]
    terms = lax.all_to_all(product.reshape(nh * nl, quarter, cols), ("yh", "yl"), 0, 0)
    keep, send = call(
        halve_kernel, [shape((eighth, cols), BF16)] * 2, [SMEM, VMEM], nh * nl * quarter * cols, 2 * half * cols, [own[1], own[-1]]
    )(place, terms)
    copies = call(
        add_kernel, shape((nz, eighth, cols), BF16), [VMEM, VMEM], eighth * cols, 2 * nz * eighth * cols
    )(keep, lax.ppermute(send, "zp", SWAP))
    scale = float(total_tokens) ** -0.5
    copies = call(
        functools.partial(total_kernel, float(total_tokens) ** -0.5),
        shape((nl * np, eighth, cols), BF16),
        [VMEM],
        nz * eighth * cols,
        2 * (nz + nl * np) * eighth * cols,
    )(lax.all_to_all(copies, "z", 0, 0))

    whole = lax.all_to_all(copies, ("yl", "zp"), 0, 0).reshape(half, cols)
    own, mark = call(
        marked_stack_kernel,
        [shape((nx, nh, half, cols), BF16), shape((16, LANES), BF16)],
        [VMEM] * nx,
        0,
        4 * width * cols,
        [copies],
    )(*own)
    other = lax.ppermute(own, "c", SWAP)
    beside = lax.ppermute(whole, "c", SWAP)
    mine = call(
        dots_kernel, shape((half // LANES, LANES), F32), [SMEM, VMEM, VMEM, VMEM], 2 * half * cols, 4 * half * cols, [mark]
    )(place, whole, key_codes, scales)
    gain_part = call(
        pair_dots_kernel,
        shape((nx * nh, rows // LANES, LANES), F32),
        [SMEM, VMEM, VMEM, VMEM, VMEM],
        2 * half * cols,
        4 * half * cols,
    )(place, mine, beside, key_codes, scales)
    gain_gradient = lax.all_to_all(gain_part, ("x", "yh"), 0, 0).reshape(width)
    weight_grad = call(
        finish_kernel, shape((rows, cols), BF16), [SMEM, VMEM, VMEM, VMEM], rows * cols, 4 * rows * cols, [gain_part]
    )(place, whole, beside, gain)
    keys_out, input_gradient = call(
        tokens_kernel,
        [shape((tok, cols), BF16), shape((tok, width), BF16)],
        [SMEM, VMEM, VMEM, VMEM, VMEM],
        4 * tok * width * cols,
        4 * tok * width + 2 * width * cols,
        [gain_part],
    )(place, hidden_in, key_cotangent, own, other)
    gain_gradient, keys_out = tie(gain_gradient, keys_out)
    return (keys_out, input_gradient, weight_grad, gain_gradient)


def solution(mesh):
    axes = ("x", "yh", "yl", "z", "zp", "c")
    fine = Mesh(mesh.devices.reshape(4, 2, 4, 6, 2, 2), axes)
    tokens = P(axes, None)
    group = ("x", "yh")
    in_specs = (tokens, P(group), P(group, None), P(group, None), tokens)
    out_specs = (tokens, tokens, P(group, None), P())
    return jax.shard_map(body, mesh=fine, in_specs=in_specs, out_specs=out_specs, check_vma=False)
```

```python
import functools

import jax
import jax.numpy as jnp
from jax import lax
from jax.experimental import pallas as pl
from jax.experimental.pallas import tpu as pltpu
from jax.sharding import Mesh
from jax.sharding import PartitionSpec as P

F32 = jnp.float32
BF16 = jnp.bfloat16
VMEM = pl.BlockSpec(memory_space=pltpu.VMEM)
SMEM = pl.BlockSpec(memory_space=pltpu.SMEM)
HBM = pl.BlockSpec(memory_space=pltpu.HBM)
PARAMS = pltpu.CompilerParams(vmem_limit_bytes=12 * 1024 * 1024)
SWAP = [(0, 1), (1, 0)]
LANES = 128


def shape(dims, dtype):
    return jax.ShapeDtypeStruct(dims, dtype)


def down(row):
    return jnp.broadcast_to(row, (LANES, row.shape[1])).T


def gained_kernel(place_ref, codes_ref, scales_ref, gain_ref, out_ref):
    half, cols = out_ref.shape
    blocks = scales_ref.shape[0]
    rows = pl.ds(pl.multiple_of(place_ref[0] * half, half), half)
    gain = gain_ref[:, rows].astype(F32)
    for b in range(blocks):
        factor = down(scales_ref[b : b + 1, rows].astype(F32) * gain)
        for at in range(b * cols // blocks, (b + 1) * cols // blocks, LANES):
            columns = slice(at, at + LANES)
            out_ref[:, columns] = (codes_ref[rows, columns].astype(F32) * factor).astype(BF16)


def prepare_kernel(hidden_ref, cot_ref, sent_ref, mark_ref, hidden, cot, come, go):
    peers, tok, part = hidden.shape
    loads = [
        pltpu.make_async_copy(hidden_ref.at[:, pl.ds(i * part, part)], hidden.at[i], come.at[i]) for i in range(peers)
    ]
    loads.append(pltpu.make_async_copy(cot_ref, cot, come.at[peers]))
    for load in loads:
        load.start()
    stores = []
    square = jnp.zeros((tok, 1), F32)
    for i in range(peers):
        loads[i].wait()
        stores.append(pltpu.make_async_copy(hidden.at[i], sent_ref.at[i, :, pl.ds(0, part)], go.at[i]))
        stores[-1].start()
        piece = hidden[i].astype(F32)
        square = square + jnp.sum(piece * piece, axis=1, keepdims=True)
    inv = lax.rsqrt(square / (peers * part) + 1e-05)
    loads[peers].wait()
    cot[...] = (cot[...].astype(F32) * inv).astype(BF16)
    for i in range(peers):
        stores.append(pltpu.make_async_copy(cot, sent_ref.at[i, :, pl.ds(part, cot.shape[1])], go.at[peers + i]))
        stores[-1].start()
    mark_ref[...] = square[:8]
    for store in stores:
        store.wait()


def stack_kernel(*refs):
    for i, ref in enumerate(refs[:-1]):
        refs[-1][i] = ref[...]


def product_kernel(place_ref, got_ref, keep_ref, send_ref):
    peers, tok, wide = got_ref.shape
    groups, half, cols = keep_ref.shape
    part = wide - cols
    core = place_ref[0]
    cot = got_ref[:, :, part:].reshape(peers * tok, cols)
    for out_ref, which in ((send_ref, 1 - core), (keep_ref, core)):
        for g in range(groups):
            at = pl.multiple_of(g * 2 * half + which * half, half)
            left = got_ref[:, :, pl.ds(at, half)].reshape(peers * tok, half)
            value = lax.dot_general(left, cot, (((0,), (0,)), ((), ())), preferred_element_type=F32)
            out_ref[g] = value.astype(out_ref.dtype)


def marked_stack_kernel(*refs):
    stack_kernel(*refs[:-1])
    refs[-1][...] = refs[0][0, :16, :LANES]


def row_dots(at, total_ref, codes_ref, scales_ref):
    half, cols = total_ref.shape
    blocks = scales_ref.shape[0]
    rows = pl.ds(pl.multiple_of(at, half), half)
    dots = jnp.zeros((half, LANES), F32)
    for b in range(blocks):
        scale = down(scales_ref[b : b + 1, rows].astype(F32))
        for c in range(b * cols // blocks, (b + 1) * cols // blocks, LANES):
            columns = slice(c, c + LANES)
            weight = (codes_ref[rows, columns].astype(F32) * scale).astype(BF16)
            dots = dots + total_ref[:, columns].astype(F32) * weight.astype(F32)
    parts = [dots[i : i + LANES].T for i in range(0, half, LANES)]
    return [jnp.sum(part, axis=0, keepdims=True) for part in parts]


def dots_kernel(place_ref, total_ref, codes_ref, scales_ref, part_ref):
    for i, row in enumerate(row_dots(place_ref[0] * total_ref.shape[0], total_ref, codes_ref, scales_ref)):
        part_ref[i : i + 1, :] = row


def pair_dots_kernel(place_ref, own_ref, total_ref, codes_ref, scales_ref, part_ref):
    core = place_ref[0]
    deep = own_ref.shape[0]
    found = row_dots((1 - core) * total_ref.shape[0], total_ref, codes_ref, scales_ref)
    for peer in range(part_ref.shape[0]):
        part_ref[peer, pl.ds(core * deep, deep), :] = own_ref[...]
        for i, row in enumerate(found):
            part_ref[peer, pl.ds((1 - core) * deep + i, 1), :] = row


def finish_kernel(place_ref, own_ref, other_ref, gain_ref, grad_ref):
    half, cols = own_ref.shape
    core = place_ref[0]
    for ref, which in ((own_ref, core), (other_ref, 1 - core)):
        rows = pl.ds(pl.multiple_of(which * half, half), half)
        gain = down(gain_ref[:, rows].astype(F32))
        for at in range(0, cols, LANES):
            columns = slice(at, at + LANES)
            grad_ref[rows, columns] = (ref[:, columns].astype(F32) * gain).astype(BF16)


def tokens_kernel(place_ref, hidden_ref, cot_ref, own_ref, other_ref, keys_ref, grad_ref):
    shifts, pairs, half, cols = own_ref.shape
    width = hidden_ref.shape[1]
    core, here, side = place_ref[0], place_ref[1], place_ref[2]
    square = jnp.zeros((hidden_ref.shape[0], 1), F32)
    for at in range(0, width, width // 4):
        piece = hidden_ref[:, at : at + width // 4].astype(F32)
        square = square + jnp.sum(piece * piece, axis=1, keepdims=True)
    inv = lax.rsqrt(square / width + 1e-05)
    cot = cot_ref[...]
    places = []
    for s in range(shifts):
        x = lax.rem(here - s + shifts, shifts)
        for j in range(pairs):
            y = lax.rem(side + j, pairs)
            for ref, which in ((own_ref, core), (other_ref, 1 - core)):
                at = pl.multiple_of(((x * pairs + y) * 2 + which) * half, half)
                places.append((ref.at[s, j], pl.ds(at, half)))
    keys = jnp.zeros(keys_ref.shape, F32)
    for ref, columns in places:
        keys = keys + jnp.dot(hidden_ref[:, columns], ref[...], preferred_element_type=F32)
    keys = keys * inv
    keys_ref[...] = keys.astype(BF16)
    mean = jnp.sum(keys * cot.astype(F32), axis=1, keepdims=True) / width
    for ref, columns in places:
        value = lax.dot_general(cot, ref[...], (((1,), (1,)), ((), ())), preferred_element_type=F32)
        unit = hidden_ref[:, columns].astype(F32) * inv
        grad_ref[:, columns] = (inv * (value - unit * mean)).astype(BF16)


def total_kernel(scale, terms_ref, copies_ref):
    total = terms_ref[0].astype(F32)
    for i in range(1, terms_ref.shape[0]):
        total = total + terms_ref[i].astype(F32)
    total = (total if scale == 1 else total * scale).astype(BF16)
    for i in range(copies_ref.shape[0]):
        copies_ref[i] = total


def call(kernel, outs, specs, flops, moved, after=()):
    count = len(specs)

    def run(*refs):
        kernel(*refs[:count], *refs[count + len(after) :])

    made = pl.pallas_call(
        run,
        out_shape=outs,
        in_specs=specs + [pl.BlockSpec(memory_space=pl.ANY)] * len(after),
        out_specs=jax.tree.map(lambda _: VMEM, outs),
        compiler_params=PARAMS,
        cost_estimate=pl.CostEstimate(flops=flops, bytes_accessed=moved, transcendentals=0),
    )
    return lambda *operands: made(*operands, *after)


def tie(*values):
    return lax.optimization_barrier(values)


def body(hidden_in, norm_gain, key_codes, key_scales, key_cotangent):
    nx, nh, nl, nz, nn, nc = (lax.axis_size(a) for a in ("x", "yh", "yl", "z", "zn", "c"))
    tok, width = hidden_in.shape
    rows, cols = key_codes.shape
    total_tokens = tok * nx * nh * nl * nz * nn * nc
    half = rows // nc
    part = width // nx
    place = jnp.stack([lax.axis_index(a) for a in ("c", "x", "yh")]).astype(jnp.int32)
    scales, gain = key_scales.T, norm_gain[None]

    sent, mark = pl.pallas_call(
        prepare_kernel,
        out_shape=[shape((nx, tok, part + cols), BF16), shape((8, 1), F32)],
        in_specs=[HBM] * 2,
        out_specs=[HBM, VMEM],
        scratch_shapes=[
            pltpu.VMEM((nx, tok, part), BF16),
            pltpu.VMEM((tok, cols), BF16),
            pltpu.SemaphoreType.DMA((nx + 1,)),
            pltpu.SemaphoreType.DMA((2 * nx,)),
        ],
        compiler_params=pltpu.CompilerParams(vmem_limit_bytes=60 * 1024 * 1024),
        cost_estimate=pl.CostEstimate(flops=4 * tok * width, bytes_accessed=4 * tok * width, transcendentals=0),
    )(hidden_in, key_cotangent)
    got = lax.all_to_all(sent, "x", 0, 0)

    mine = call(gained_kernel, shape((half, cols), BF16), [SMEM, VMEM, VMEM, VMEM], half * cols, 4 * half * cols, [mark])(
        place, key_codes, scales, gain
    )
    mate = lax.ppermute(mine, "yh", SWAP)

    keep, send = call(
        product_kernel,
        [shape((nh, half, cols), F32), shape((nh, half, cols), BF16)],
        [SMEM, VMEM],
        2 * nx * tok * part * cols,
        2 * nx * tok * (part + cols) + 6 * nh * half * cols,
        [mate],
    )(place, got)
    product = (keep + lax.ppermute(send, "c", SWAP).astype(F32)).astype(BF16)
    pair = call(stack_kernel, shape((nh, half, cols), BF16), [VMEM] * 2, 0, 4 * nh * half * cols, [product])(mine, mate)

    quarter = half // nl
    share = quarter // nn
    own = [pair] + [lax.ppermute(pair, "x", [(i, (i + s) % nx) for i in range(nx)]) for s in range(1, nx)]
    terms = lax.all_to_all(product.reshape(nh * nl, quarter, cols), ("yh", "yl"), 0, 0)
    terms = call(
        functools.partial(total_kernel, 1.0),
        shape((1, quarter, cols), BF16),
        [VMEM],
        nh * nl * quarter * cols,
        2 * half * cols,
    )(terms)
    terms = lax.all_to_all(terms.reshape(nn, share, cols), "zn", 0, 0)
    terms = call(
        functools.partial(total_kernel, 1.0),
        shape((nz, share, cols), BF16),
        [VMEM],
        nn * share * cols,
        2 * (nn + nz) * share * cols,
        [own[1], own[-1]],
    )(terms)
    copies = call(
        functools.partial(total_kernel, float(total_tokens) ** -0.5),
        shape((nl * nn, share, cols), BF16),
        [VMEM],
        nz * share * cols,
        2 * (nz + nl * nn) * share * cols,
    )(lax.all_to_all(terms, "z", 0, 0))

    whole = lax.all_to_all(copies, ("yl", "zn"), 0, 0).reshape(half, cols)
    own, mark = call(
        marked_stack_kernel,
        [shape((nx, nh, half, cols), BF16), shape((16, LANES), BF16)],
        [VMEM] * nx,
        0,
        4 * width * cols,
        [copies],
    )(*own)
    other = lax.ppermute(own, "c", SWAP)
    beside = lax.ppermute(whole, "c", SWAP)
    mine = call(
        dots_kernel, shape((half // LANES, LANES), F32), [SMEM, VMEM, VMEM, VMEM], 2 * half * cols, 4 * half * cols, [mark]
    )(place, whole, key_codes, scales)
    gain_part = call(
        pair_dots_kernel,
        shape((nx * nh, rows // LANES, LANES), F32),
        [SMEM, VMEM, VMEM, VMEM, VMEM],
        2 * half * cols,
        4 * half * cols,
    )(place, mine, beside, key_codes, scales)
    gain_gradient = lax.all_to_all(gain_part, ("x", "yh"), 0, 0).reshape(width)
    weight_grad = call(
        finish_kernel, shape((rows, cols), BF16), [SMEM, VMEM, VMEM, VMEM], rows * cols, 4 * rows * cols, [gain_part]
    )(place, whole, beside, gain)
    keys_out, input_gradient = call(
        tokens_kernel,
        [shape((tok, cols), BF16), shape((tok, width), BF16)],
        [SMEM, VMEM, VMEM, VMEM, VMEM],
        4 * tok * width * cols,
        4 * tok * width + 2 * width * cols,
        [gain_part],
    )(place, hidden_in, key_cotangent, own, other)
    gain_gradient, keys_out = tie(gain_gradient, keys_out)
    return (keys_out, input_gradient, weight_grad, gain_gradient)


def solution(mesh):
    axes = ("x", "yh", "yl", "z", "zn", "c")
    fine = Mesh(mesh.devices.reshape(4, 2, 4, 3, 4, 2), axes)
    tokens = P(axes, None)
    group = ("x", "yh")
    in_specs = (tokens, P(group), P(group, None), P(group, None), tokens)
    out_specs = (tokens, tokens, P(group, None), P())
    return jax.shard_map(body, mesh=fine, in_specs=in_specs, out_specs=out_specs, check_vma=False)
```

```python
import functools

import jax
import jax.numpy as jnp
from jax import lax
from jax.experimental import pallas as pl
from jax.experimental.pallas import tpu as pltpu
from jax.sharding import Mesh
from jax.sharding import PartitionSpec as P

F32 = jnp.float32
BF16 = jnp.bfloat16
VMEM = pl.BlockSpec(memory_space=pltpu.VMEM)
SMEM = pl.BlockSpec(memory_space=pltpu.SMEM)
HBM = pl.BlockSpec(memory_space=pltpu.HBM)
PARAMS = pltpu.CompilerParams(vmem_limit_bytes=12 * 1024 * 1024)
SWAP = [(0, 1), (1, 0)]
LANES = 128


def shape(dims, dtype):
    return jax.ShapeDtypeStruct(dims, dtype)


def down(row):
    return jnp.broadcast_to(row, (LANES, row.shape[1])).T


def gained_kernel(place_ref, codes_ref, scales_ref, gain_ref, out_ref):
    half, cols = out_ref.shape
    blocks = scales_ref.shape[0]
    rows = pl.ds(pl.multiple_of(place_ref[0] * half, half), half)
    gain = gain_ref[:, rows].astype(F32)
    for b in range(blocks):
        factor = down(scales_ref[b : b + 1, rows].astype(F32) * gain)
        for at in range(b * cols // blocks, (b + 1) * cols // blocks, LANES):
            columns = slice(at, at + LANES)
            out_ref[:, columns] = (codes_ref[rows, columns].astype(F32) * factor).astype(BF16)


def prepare_kernel(hidden_ref, cot_ref, sent_ref, mark_ref, hidden, cot, come, go):
    peers, tok, part = hidden.shape
    loads = [
        pltpu.make_async_copy(hidden_ref.at[:, pl.ds(i * part, part)], hidden.at[i], come.at[i]) for i in range(peers)
    ]
    loads.append(pltpu.make_async_copy(cot_ref, cot, come.at[peers]))
    for load in loads:
        load.start()
    stores = [
        pltpu.make_async_copy(hidden_ref.at[:, pl.ds(i * part, part)], sent_ref.at[i, :, pl.ds(0, part)], go.at[i])
        for i in range(peers)
    ]
    for store in stores:
        store.start()
    square = jnp.zeros((tok, 1), F32)
    for i in range(peers):
        loads[i].wait()
        piece = hidden[i].astype(F32)
        square = square + jnp.sum(piece * piece, axis=1, keepdims=True)
    inv = lax.rsqrt(square / (peers * part) + 1e-05)
    loads[peers].wait()
    cot[...] = (cot[...].astype(F32) * inv).astype(BF16)
    for i in range(peers):
        stores.append(pltpu.make_async_copy(cot, sent_ref.at[i, :, pl.ds(part, cot.shape[1])], go.at[peers + i]))
        stores[-1].start()
    mark_ref[...] = square[:8]
    for store in stores:
        store.wait()


def stack_kernel(*refs):
    for i, ref in enumerate(refs[:-1]):
        refs[-1][i] = ref[...]


def product_kernel(place_ref, got_ref, keep_ref, send_ref):
    peers, tok, wide = got_ref.shape
    groups, half, cols = keep_ref.shape
    part = wide - cols
    core = place_ref[0]
    cot = got_ref[:, :, part:].reshape(peers * tok, cols)
    for out_ref, which in ((send_ref, 1 - core), (keep_ref, core)):
        for g in range(groups):
            at = pl.multiple_of(g * 2 * half + which * half, half)
            left = got_ref[:, :, pl.ds(at, half)].reshape(peers * tok, half)
            value = lax.dot_general(left, cot, (((0,), (0,)), ((), ())), preferred_element_type=F32)
            out_ref[g] = value.astype(out_ref.dtype)


def marked_stack_kernel(*refs):
    stack_kernel(*refs[:-1])
    refs[-1][...] = refs[0][0, :16, :LANES]


def row_dots(at, total_ref, codes_ref, scales_ref):
    half, cols = total_ref.shape
    blocks = scales_ref.shape[0]
    rows = pl.ds(pl.multiple_of(at, half), half)
    dots = jnp.zeros((half, LANES), F32)
    for b in range(blocks):
        scale = down(scales_ref[b : b + 1, rows].astype(F32))
        for c in range(b * cols // blocks, (b + 1) * cols // blocks, LANES):
            columns = slice(c, c + LANES)
            weight = (codes_ref[rows, columns].astype(F32) * scale).astype(BF16)
            dots = dots + total_ref[:, columns].astype(F32) * weight.astype(F32)
    parts = [dots[i : i + LANES].T for i in range(0, half, LANES)]
    return [jnp.sum(part, axis=0, keepdims=True) for part in parts]


def dots_kernel(place_ref, total_ref, codes_ref, scales_ref, part_ref):
    for i, row in enumerate(row_dots(place_ref[0] * total_ref.shape[0], total_ref, codes_ref, scales_ref)):
        part_ref[i : i + 1, :] = row


def pair_dots_kernel(place_ref, own_ref, total_ref, codes_ref, scales_ref, part_ref):
    core = place_ref[0]
    deep = own_ref.shape[0]
    found = row_dots((1 - core) * total_ref.shape[0], total_ref, codes_ref, scales_ref)
    for peer in range(part_ref.shape[0]):
        part_ref[peer, pl.ds(core * deep, deep), :] = own_ref[...]
        for i, row in enumerate(found):
            part_ref[peer, pl.ds((1 - core) * deep + i, 1), :] = row


def finish_kernel(place_ref, own_ref, other_ref, gain_ref, grad_ref):
    half, cols = own_ref.shape
    core = place_ref[0]
    for ref, which in ((own_ref, core), (other_ref, 1 - core)):
        rows = pl.ds(pl.multiple_of(which * half, half), half)
        gain = down(gain_ref[:, rows].astype(F32))
        for at in range(0, cols, LANES):
            columns = slice(at, at + LANES)
            grad_ref[rows, columns] = (ref[:, columns].astype(F32) * gain).astype(BF16)


def tokens_kernel(place_ref, hidden_ref, cot_ref, own_ref, other_ref, keys_ref, grad_ref):
    shifts, pairs, half, cols = own_ref.shape
    width = hidden_ref.shape[1]
    core, here, side = place_ref[0], place_ref[1], place_ref[2]
    square = jnp.zeros((hidden_ref.shape[0], 1), F32)
    for at in range(0, width, width // 4):
        piece = hidden_ref[:, at : at + width // 4].astype(F32)
        square = square + jnp.sum(piece * piece, axis=1, keepdims=True)
    inv = lax.rsqrt(square / width + 1e-05)
    cot = cot_ref[...]
    places = []
    for s in range(shifts):
        x = lax.rem(here - s + shifts, shifts)
        for j in range(pairs):
            y = lax.rem(side + j, pairs)
            for ref, which in ((own_ref, core), (other_ref, 1 - core)):
                at = pl.multiple_of(((x * pairs + y) * 2 + which) * half, half)
                places.append((ref.at[s, j], pl.ds(at, half)))
    keys = jnp.zeros(keys_ref.shape, F32)
    for ref, columns in places:
        keys = keys + jnp.dot(hidden_ref[:, columns], ref[...], preferred_element_type=F32)
    keys = keys * inv
    keys_ref[...] = keys.astype(BF16)
    mean = jnp.sum(keys * cot.astype(F32), axis=1, keepdims=True) / width
    for ref, columns in places:
        value = lax.dot_general(cot, ref[...], (((1,), (1,)), ((), ())), preferred_element_type=F32)
        unit = hidden_ref[:, columns].astype(F32) * inv
        grad_ref[:, columns] = (inv * (value - unit * mean)).astype(BF16)


def total_kernel(scale, terms_ref, copies_ref):
    total = terms_ref[0].astype(F32)
    for i in range(1, terms_ref.shape[0]):
        total = total + terms_ref[i].astype(F32)
    total = (total if scale == 1 else total * scale).astype(BF16)
    for i in range(copies_ref.shape[0]):
        copies_ref[i] = total


def call(kernel, outs, specs, flops, moved, after=()):
    count = len(specs)

    def run(*refs):
        kernel(*refs[:count], *refs[count + len(after) :])

    made = pl.pallas_call(
        run,
        out_shape=outs,
        in_specs=specs + [pl.BlockSpec(memory_space=pl.ANY)] * len(after),
        out_specs=jax.tree.map(lambda _: VMEM, outs),
        compiler_params=PARAMS,
        cost_estimate=pl.CostEstimate(flops=flops, bytes_accessed=moved, transcendentals=0),
    )
    return lambda *operands: made(*operands, *after)


def tie(*values):
    return lax.optimization_barrier(values)


def body(hidden_in, norm_gain, key_codes, key_scales, key_cotangent):
    nx, nh, nl, nz, np, nc = (lax.axis_size(a) for a in ("x", "yh", "yl", "z", "zp", "c"))
    tok, width = hidden_in.shape
    rows, cols = key_codes.shape
    total_tokens = tok * nx * nh * nl * nz * np * nc
    half = rows // nc
    part = width // nx
    place = jnp.stack([lax.axis_index(a) for a in ("c", "x", "yh")]).astype(jnp.int32)
    scales, gain = key_scales.T, norm_gain[None]

    sent, mark = pl.pallas_call(
        prepare_kernel,
        out_shape=[shape((nx, tok, part + cols), BF16), shape((8, 1), F32)],
        in_specs=[HBM] * 2,
        out_specs=[HBM, VMEM],
        scratch_shapes=[
            pltpu.VMEM((nx, tok, part), BF16),
            pltpu.VMEM((tok, cols), BF16),
            pltpu.SemaphoreType.DMA((nx + 1,)),
            pltpu.SemaphoreType.DMA((2 * nx,)),
        ],
        compiler_params=pltpu.CompilerParams(vmem_limit_bytes=60 * 1024 * 1024),
        cost_estimate=pl.CostEstimate(flops=4 * tok * width, bytes_accessed=4 * tok * width, transcendentals=0),
    )(hidden_in, key_cotangent)
    got = lax.all_to_all(sent, "x", 0, 0)

    mine = call(gained_kernel, shape((half, cols), BF16), [SMEM, VMEM, VMEM, VMEM], half * cols, 4 * half * cols, [mark])(
        place, key_codes, scales, gain
    )
    mate = lax.ppermute(mine, "yh", SWAP)

    keep, send = call(
        product_kernel,
        [shape((nh, half, cols), F32), shape((nh, half, cols), BF16)],
        [SMEM, VMEM],
        2 * nx * tok * part * cols,
        2 * nx * tok * (part + cols) + 6 * nh * half * cols,
        [mate],
    )(place, got)
    product = (keep + lax.ppermute(send, "c", SWAP).astype(F32)).astype(BF16)
    pair = call(stack_kernel, shape((nh, half, cols), BF16), [VMEM] * 2, 0, 4 * nh * half * cols, [product])(mine, mate)

    quarter = half // nl
    eighth = quarter // np
    own = [pair] + [lax.ppermute(pair, "x", [(i, (i + s) % nx) for i in range(nx)]) for s in range(1, nx)]
    terms = lax.all_to_all(product.reshape(nh * nl * np, eighth, cols), ("yh", "yl", "zp"), 0, 0)
    copies = call(
        functools.partial(total_kernel, 1.0),
        shape((nz, eighth, cols), BF16),
        [VMEM],
        nh * nl * quarter * cols,
        2 * (nh * nl * np + nz) * eighth * cols,
        [own[1]],
    )(terms)
    copies = call(
        functools.partial(total_kernel, float(total_tokens) ** -0.5),
        shape((nl * np, eighth, cols), BF16),
        [VMEM],
        nz * eighth * cols,
        2 * (nz + nl * np) * eighth * cols,
    )(lax.all_to_all(copies, "z", 0, 0))

    whole = lax.all_to_all(copies, ("yl", "zp"), 0, 0).reshape(half, cols)
    own, mark = call(
        marked_stack_kernel,
        [shape((nx, nh, half, cols), BF16), shape((16, LANES), BF16)],
        [VMEM] * nx,
        0,
        4 * width * cols,
        [copies],
    )(*own)
    other = lax.ppermute(own, "c", SWAP)
    beside = lax.ppermute(whole, "c", SWAP)
    mine = call(
        dots_kernel, shape((half // LANES, LANES), F32), [SMEM, VMEM, VMEM, VMEM], 2 * half * cols, 4 * half * cols, [mark]
    )(place, whole, key_codes, scales)
    gain_part = call(
        pair_dots_kernel,
        shape((nx * nh, rows // LANES, LANES), F32),
        [SMEM, VMEM, VMEM, VMEM, VMEM],
        2 * half * cols,
        4 * half * cols,
    )(place, mine, beside, key_codes, scales)
    gain_gradient = lax.all_to_all(gain_part, ("x", "yh"), 0, 0).reshape(width)
    weight_grad = call(
        finish_kernel, shape((rows, cols), BF16), [SMEM, VMEM, VMEM, VMEM], rows * cols, 4 * rows * cols, [gain_part]
    )(place, whole, beside, gain)
    keys_out, input_gradient = call(
        tokens_kernel,
        [shape((tok, cols), BF16), shape((tok, width), BF16)],
        [SMEM, VMEM, VMEM, VMEM, VMEM],
        4 * tok * width * cols,
        4 * tok * width + 2 * width * cols,
        [gain_part],
    )(place, hidden_in, key_cotangent, own, other)
    gain_gradient, keys_out = tie(gain_gradient, keys_out)
    return (keys_out, input_gradient, weight_grad, gain_gradient)


def solution(mesh):
    axes = ("x", "yh", "yl", "z", "zp", "c")
    fine = Mesh(mesh.devices.reshape(4, 2, 4, 6, 2, 2), axes)
    tokens = P(axes, None)
    group = ("x", "yh")
    in_specs = (tokens, P(group), P(group, None), P(group, None), tokens)
    out_specs = (tokens, tokens, P(group, None), P())
    return jax.shard_map(body, mesh=fine, in_specs=in_specs, out_specs=out_specs, check_vma=False)
```

```python
import functools

import jax
import jax.numpy as jnp
from jax import lax
from jax.experimental import pallas as pl
from jax.experimental.pallas import tpu as pltpu
from jax.sharding import Mesh
from jax.sharding import PartitionSpec as P

F32 = jnp.float32
BF16 = jnp.bfloat16
VMEM = pl.BlockSpec(memory_space=pltpu.VMEM)
SMEM = pl.BlockSpec(memory_space=pltpu.SMEM)
HBM = pl.BlockSpec(memory_space=pltpu.HBM)
PARAMS = pltpu.CompilerParams(vmem_limit_bytes=12 * 1024 * 1024)
SWAP = [(0, 1), (1, 0)]
LANES = 128


def shape(dims, dtype):
    return jax.ShapeDtypeStruct(dims, dtype)


def down(row):
    return jnp.broadcast_to(row, (LANES, row.shape[1])).T


def gained_kernel(place_ref, codes_ref, scales_ref, gain_ref, out_ref):
    half, cols = out_ref.shape
    blocks = scales_ref.shape[0]
    rows = pl.ds(pl.multiple_of(place_ref[0] * half, half), half)
    gain = gain_ref[:, rows].astype(F32)
    for b in range(blocks):
        factor = down(scales_ref[b : b + 1, rows].astype(F32) * gain)
        for at in range(b * cols // blocks, (b + 1) * cols // blocks, LANES):
            columns = slice(at, at + LANES)
            out_ref[:, columns] = (codes_ref[rows, columns].astype(F32) * factor).astype(BF16)


def prepare_kernel(hidden_ref, cot_ref, sent_ref, mark_ref, hidden, cot, come, go):
    peers, tok, part = hidden.shape
    loads = [
        pltpu.make_async_copy(hidden_ref.at[:, pl.ds(i * part, part)], hidden.at[i], come.at[i]) for i in range(peers)
    ]
    loads.append(pltpu.make_async_copy(cot_ref, cot, come.at[peers]))
    for load in loads:
        load.start()
    stores = []
    square = jnp.zeros((tok, 1), F32)
    for i in range(peers):
        loads[i].wait()
        stores.append(pltpu.make_async_copy(hidden.at[i], sent_ref.at[i, :, pl.ds(0, part)], go.at[i]))
        stores[-1].start()
        piece = hidden[i].astype(F32)
        square = square + jnp.sum(piece * piece, axis=1, keepdims=True)
    inv = lax.rsqrt(square / (peers * part) + 1e-05)
    loads[peers].wait()
    cot[...] = (cot[...].astype(F32) * inv).astype(BF16)
    for i in range(peers):
        stores.append(pltpu.make_async_copy(cot, sent_ref.at[i, :, pl.ds(part, cot.shape[1])], go.at[peers + i]))
        stores[-1].start()
    mark_ref[...] = square[:8]
    for store in stores:
        store.wait()


def stack_kernel(*refs):
    for i, ref in enumerate(refs[:-1]):
        refs[-1][i] = ref[...]


def product_kernel(place_ref, got_ref, keep_ref, send_ref):
    peers, tok, wide = got_ref.shape
    groups, half, cols = keep_ref.shape
    part = wide - cols
    core = place_ref[0]
    cot = got_ref[:, :, part:].reshape(peers * tok, cols)
    for out_ref, which in ((send_ref, 1 - core), (keep_ref, core)):
        for g in range(groups):
            at = pl.multiple_of(g * 2 * half + which * half, half)
            left = got_ref[:, :, pl.ds(at, half)].reshape(peers * tok, half)
            value = lax.dot_general(left, cot, (((0,), (0,)), ((), ())), preferred_element_type=F32)
            out_ref[g] = value.astype(out_ref.dtype)


def marked_stack_kernel(*refs):
    stack_kernel(*refs[:-1])
    refs[-1][...] = refs[0][0, :16, :LANES]


def row_dots(at, total_ref, codes_ref, scales_ref):
    half, cols = total_ref.shape
    blocks = scales_ref.shape[0]
    rows = pl.ds(pl.multiple_of(at, half), half)
    dots = jnp.zeros((half, LANES), F32)
    for b in range(blocks):
        scale = down(scales_ref[b : b + 1, rows].astype(F32))
        for c in range(b * cols // blocks, (b + 1) * cols // blocks, LANES):
            columns = slice(c, c + LANES)
            weight = (codes_ref[rows, columns].astype(F32) * scale).astype(BF16)
            dots = dots + total_ref[:, columns].astype(F32) * weight.astype(F32)
    parts = [dots[i : i + LANES].T for i in range(0, half, LANES)]
    return [jnp.sum(part, axis=0, keepdims=True) for part in parts]


def dots_kernel(place_ref, total_ref, codes_ref, scales_ref, part_ref):
    for i, row in enumerate(row_dots(place_ref[0] * total_ref.shape[0], total_ref, codes_ref, scales_ref)):
        part_ref[i : i + 1, :] = row


def pair_dots_kernel(place_ref, own_ref, total_ref, codes_ref, scales_ref, part_ref):
    core = place_ref[0]
    deep = own_ref.shape[0]
    found = row_dots((1 - core) * total_ref.shape[0], total_ref, codes_ref, scales_ref)
    for peer in range(part_ref.shape[0]):
        part_ref[peer, pl.ds(core * deep, deep), :] = own_ref[...]
        for i, row in enumerate(found):
            part_ref[peer, pl.ds((1 - core) * deep + i, 1), :] = row


def finish_kernel(place_ref, own_ref, other_ref, gain_ref, grad_ref):
    half, cols = own_ref.shape
    core = place_ref[0]
    for ref, which in ((own_ref, core), (other_ref, 1 - core)):
        rows = pl.ds(pl.multiple_of(which * half, half), half)
        gain = down(gain_ref[:, rows].astype(F32))
        for at in range(0, cols, LANES):
            columns = slice(at, at + LANES)
            grad_ref[rows, columns] = (ref[:, columns].astype(F32) * gain).astype(BF16)


def tokens_kernel(place_ref, hidden_ref, cot_ref, own_ref, other_ref, keys_ref, grad_ref):
    shifts, pairs, half, cols = own_ref.shape
    width = hidden_ref.shape[1]
    core, here, side = place_ref[0], place_ref[1], place_ref[2]
    square = jnp.zeros((hidden_ref.shape[0], 1), F32)
    for at in range(0, width, width // 4):
        piece = hidden_ref[:, at : at + width // 4].astype(F32)
        square = square + jnp.sum(piece * piece, axis=1, keepdims=True)
    inv = lax.rsqrt(square / width + 1e-05)
    cot = cot_ref[...]
    places = []
    for s in range(shifts):
        x = lax.rem(here - s + shifts, shifts)
        for j in range(pairs):
            y = lax.rem(side + j, pairs)
            for ref, which in ((own_ref, core), (other_ref, 1 - core)):
                at = pl.multiple_of(((x * pairs + y) * 2 + which) * half, half)
                places.append((ref.at[s, j], pl.ds(at, half)))
    keys = jnp.zeros(keys_ref.shape, F32)
    for ref, columns in places:
        keys = keys + jnp.dot(hidden_ref[:, columns], ref[...], preferred_element_type=F32)
    keys = keys * inv
    keys_ref[...] = keys.astype(BF16)
    mean = jnp.sum(keys * cot.astype(F32), axis=1, keepdims=True) / width
    for ref, columns in places:
        value = lax.dot_general(cot, ref[...], (((1,), (1,)), ((), ())), preferred_element_type=F32)
        unit = hidden_ref[:, columns].astype(F32) * inv
        grad_ref[:, columns] = (inv * (value - unit * mean)).astype(BF16)


def total_kernel(scale, terms_ref, copies_ref):
    total = terms_ref[0].astype(F32)
    for i in range(1, terms_ref.shape[0]):
        total = total + terms_ref[i].astype(F32)
    total = (total if scale == 1 else total * scale).astype(BF16)
    for i in range(copies_ref.shape[0]):
        copies_ref[i] = total


def call(kernel, outs, specs, flops, moved, after=()):
    count = len(specs)

    def run(*refs):
        kernel(*refs[:count], *refs[count + len(after) :])

    made = pl.pallas_call(
        run,
        out_shape=outs,
        in_specs=specs + [pl.BlockSpec(memory_space=pl.ANY)] * len(after),
        out_specs=jax.tree.map(lambda _: VMEM, outs),
        compiler_params=PARAMS,
        cost_estimate=pl.CostEstimate(flops=flops, bytes_accessed=moved, transcendentals=0),
    )
    return lambda *operands: made(*operands, *after)


def tie(*values):
    return lax.optimization_barrier(values)


def body(hidden_in, norm_gain, key_codes, key_scales, key_cotangent):
    nx, nh, nl, nz, np, nc = (lax.axis_size(a) for a in ("x", "yh", "yl", "z", "zp", "c"))
    tok, width = hidden_in.shape
    rows, cols = key_codes.shape
    total_tokens = tok * nx * nh * nl * nz * np * nc
    half = rows // nc
    part = width // nx
    place = jnp.stack([lax.axis_index(a) for a in ("c", "x", "yh")]).astype(jnp.int32)
    scales, gain = key_scales.T, norm_gain[None]

    sent, mark = pl.pallas_call(
        prepare_kernel,
        out_shape=[shape((nx, tok, part + cols), BF16), shape((8, 1), F32)],
        in_specs=[HBM] * 2,
        out_specs=[HBM, VMEM],
        scratch_shapes=[
            pltpu.VMEM((nx, tok, part), BF16),
            pltpu.VMEM((tok, cols), BF16),
            pltpu.SemaphoreType.DMA((nx + 1,)),
            pltpu.SemaphoreType.DMA((2 * nx,)),
        ],
        compiler_params=pltpu.CompilerParams(vmem_limit_bytes=60 * 1024 * 1024),
        cost_estimate=pl.CostEstimate(flops=4 * tok * width, bytes_accessed=4 * tok * width, transcendentals=0),
    )(hidden_in, key_cotangent)
    got = lax.all_to_all(sent, "x", 0, 0)

    mine = call(gained_kernel, shape((half, cols), BF16), [SMEM, VMEM, VMEM, VMEM], half * cols, 4 * half * cols, [mark])(
        place, key_codes, scales, gain
    )
    mate = lax.ppermute(mine, "yh", SWAP)

    keep, send = call(
        product_kernel,
        [shape((nh, half, cols), F32), shape((nh, half, cols), BF16)],
        [SMEM, VMEM],
        2 * nx * tok * part * cols,
        2 * nx * tok * (part + cols) + 6 * nh * half * cols,
        [mate],
    )(place, got)
    product = (keep + lax.ppermute(send, "c", SWAP).astype(F32)).astype(BF16)
    pair = call(stack_kernel, shape((nh, half, cols), BF16), [VMEM] * 2, 0, 4 * nh * half * cols, [product])(mine, mate)

    quarter = half // nl
    eighth = quarter // np
    own = [pair] + [lax.ppermute(pair, "x", [(i, (i + s) % nx) for i in range(nx)]) for s in range(1, nx)]
    terms = lax.all_to_all(product.reshape(nh * nl * np, eighth, cols), ("yh", "yl", "zp"), 0, 0)
    copies = call(
        functools.partial(total_kernel, 1.0),
        shape((nz, eighth, cols), BF16),
        [VMEM],
        nh * nl * quarter * cols,
        2 * (nh * nl * np + nz) * eighth * cols,
    )(terms)
    copies = call(
        functools.partial(total_kernel, float(total_tokens) ** -0.5),
        shape((nl * np, eighth, cols), BF16),
        [VMEM],
        nz * eighth * cols,
        2 * (nz + nl * np) * eighth * cols,
        own[1:],
    )(lax.all_to_all(copies, "z", 0, 0))

    whole = lax.all_to_all(copies, ("yl", "zp"), 0, 0).reshape(half, cols)
    own, mark = call(
        marked_stack_kernel,
        [shape((nx, nh, half, cols), BF16), shape((16, LANES), BF16)],
        [VMEM] * nx,
        0,
        4 * width * cols,
        [copies],
    )(*own)
    other = lax.ppermute(own, "c", SWAP)
    beside = lax.ppermute(whole, "c", SWAP)
    mine = call(
        dots_kernel, shape((half // LANES, LANES), F32), [SMEM, VMEM, VMEM, VMEM], 2 * half * cols, 4 * half * cols, [mark]
    )(place, whole, key_codes, scales)
    gain_part = call(
        pair_dots_kernel,
        shape((nx * nh, rows // LANES, LANES), F32),
        [SMEM, VMEM, VMEM, VMEM, VMEM],
        2 * half * cols,
        4 * half * cols,
    )(place, mine, beside, key_codes, scales)
    gain_gradient = lax.all_to_all(gain_part, ("x", "yh"), 0, 0).reshape(width)
    weight_grad = call(
        finish_kernel, shape((rows, cols), BF16), [SMEM, VMEM, VMEM, VMEM], rows * cols, 4 * rows * cols, [gain_part]
    )(place, whole, beside, gain)
    keys_out, input_gradient = call(
        tokens_kernel,
        [shape((tok, cols), BF16), shape((tok, width), BF16)],
        [SMEM, VMEM, VMEM, VMEM, VMEM],
        4 * tok * width * cols,
        4 * tok * width + 2 * width * cols,
        [gain_part],
    )(place, hidden_in, key_cotangent, own, other)
    gain_gradient, keys_out = tie(gain_gradient, keys_out)
    return (keys_out, input_gradient, weight_grad, gain_gradient)


def solution(mesh):
    axes = ("x", "yh", "yl", "z", "zp", "c")
    fine = Mesh(mesh.devices.reshape(4, 2, 4, 6, 2, 2), axes)
    tokens = P(axes, None)
    group = ("x", "yh")
    in_specs = (tokens, P(group), P(group, None), P(group, None), tokens)
    out_specs = (tokens, tokens, P(group, None), P())
    return jax.shard_map(body, mesh=fine, in_specs=in_specs, out_specs=out_specs, check_vma=False)
```

```python
import functools

import jax
import jax.numpy as jnp
from jax import lax
from jax.experimental import pallas as pl
from jax.experimental.pallas import tpu as pltpu
from jax.sharding import Mesh
from jax.sharding import PartitionSpec as P

F32 = jnp.float32
BF16 = jnp.bfloat16
VMEM = pl.BlockSpec(memory_space=pltpu.VMEM)
SMEM = pl.BlockSpec(memory_space=pltpu.SMEM)
HBM = pl.BlockSpec(memory_space=pltpu.HBM)
PARAMS = pltpu.CompilerParams(vmem_limit_bytes=12 * 1024 * 1024)
SWAP = [(0, 1), (1, 0)]
LANES = 128


def shape(dims, dtype):
    return jax.ShapeDtypeStruct(dims, dtype)


def down(row):
    return jnp.broadcast_to(row, (LANES, row.shape[1])).T


def gained_kernel(place_ref, codes_ref, scales_ref, gain_ref, out_ref):
    half, cols = out_ref.shape
    blocks = scales_ref.shape[0]
    rows = pl.ds(pl.multiple_of(place_ref[0] * half, half), half)
    gain = gain_ref[:, rows].astype(F32)
    for b in range(blocks):
        factor = down(scales_ref[b : b + 1, rows].astype(F32) * gain)
        for at in range(b * cols // blocks, (b + 1) * cols // blocks, LANES):
            columns = slice(at, at + LANES)
            out_ref[:, columns] = (codes_ref[rows, columns].astype(F32) * factor).astype(BF16)


def prepare_kernel(hidden_ref, cot_ref, sent_ref, mark_ref, hidden, cot, come, go):
    peers, tok, part = hidden.shape
    loads = [
        pltpu.make_async_copy(hidden_ref.at[:, pl.ds(i * part, part)], hidden.at[i], come.at[i]) for i in range(peers)
    ]
    loads.append(pltpu.make_async_copy(cot_ref, cot, come.at[peers]))
    for load in loads:
        load.start()
    stores = []
    square = jnp.zeros((tok, 1), F32)
    for i in range(peers):
        loads[i].wait()
        stores.append(pltpu.make_async_copy(hidden.at[i], sent_ref.at[i, :, pl.ds(0, part)], go.at[i]))
        stores[-1].start()
        piece = hidden[i].astype(F32)
        square = square + jnp.sum(piece * piece, axis=1, keepdims=True)
    inv = lax.rsqrt(square / (peers * part) + 1e-05)
    loads[peers].wait()
    cot[...] = (cot[...].astype(F32) * inv).astype(BF16)
    for i in range(peers):
        stores.append(pltpu.make_async_copy(cot, sent_ref.at[i, :, pl.ds(part, cot.shape[1])], go.at[peers + i]))
        stores[-1].start()
    mark_ref[...] = square[:8]
    for store in stores:
        store.wait()


def stack_kernel(*refs):
    for i, ref in enumerate(refs[:-1]):
        refs[-1][i] = ref[...]


def product_kernel(place_ref, got_ref, keep_ref, send_ref):
    peers, tok, wide = got_ref.shape
    groups, half, cols = keep_ref.shape
    part = wide - cols
    core = place_ref[0]
    cot = got_ref[:, :, part:].reshape(peers * tok, cols)
    for out_ref, which in ((send_ref, 1 - core), (keep_ref, core)):
        for g in range(groups):
            at = pl.multiple_of(g * 2 * half + which * half, half)
            left = got_ref[:, :, pl.ds(at, half)].reshape(peers * tok, half)
            value = lax.dot_general(left, cot, (((0,), (0,)), ((), ())), preferred_element_type=F32)
            out_ref[g] = value.astype(out_ref.dtype)


def marked_stack_kernel(*refs):
    stack_kernel(*refs[:-1])
    refs[-1][...] = refs[0][0, :16, :LANES]


def row_dots(at, total_ref, codes_ref, scales_ref):
    half, cols = total_ref.shape
    blocks = scales_ref.shape[0]
    rows = pl.ds(pl.multiple_of(at, half), half)
    dots = jnp.zeros((half, LANES), F32)
    for b in range(blocks):
        scale = down(scales_ref[b : b + 1, rows].astype(F32))
        for c in range(b * cols // blocks, (b + 1) * cols // blocks, LANES):
            columns = slice(c, c + LANES)
            weight = (codes_ref[rows, columns].astype(F32) * scale).astype(BF16)
            dots = dots + total_ref[:, columns].astype(F32) * weight.astype(F32)
    parts = [dots[i : i + LANES].T for i in range(0, half, LANES)]
    return [jnp.sum(part, axis=0, keepdims=True) for part in parts]


def dots_kernel(place_ref, total_ref, codes_ref, scales_ref, part_ref):
    for i, row in enumerate(row_dots(place_ref[0] * total_ref.shape[0], total_ref, codes_ref, scales_ref)):
        part_ref[i : i + 1, :] = row


def pair_dots_kernel(place_ref, own_ref, total_ref, codes_ref, scales_ref, part_ref):
    core = place_ref[0]
    deep = own_ref.shape[0]
    found = row_dots((1 - core) * total_ref.shape[0], total_ref, codes_ref, scales_ref)
    for peer in range(part_ref.shape[0]):
        part_ref[peer, pl.ds(core * deep, deep), :] = own_ref[...]
        for i, row in enumerate(found):
            part_ref[peer, pl.ds((1 - core) * deep + i, 1), :] = row


def finish_kernel(place_ref, own_ref, other_ref, gain_ref, grad_ref):
    half, cols = own_ref.shape
    core = place_ref[0]
    for ref, which in ((own_ref, core), (other_ref, 1 - core)):
        rows = pl.ds(pl.multiple_of(which * half, half), half)
        gain = down(gain_ref[:, rows].astype(F32))
        for at in range(0, cols, LANES):
            columns = slice(at, at + LANES)
            grad_ref[rows, columns] = (ref[:, columns].astype(F32) * gain).astype(BF16)


def tokens_kernel(place_ref, hidden_ref, cot_ref, own_ref, other_ref, keys_ref, grad_ref):
    shifts, pairs, half, cols = own_ref.shape
    width = hidden_ref.shape[1]
    core, here, side = place_ref[0], place_ref[1], place_ref[2]
    square = jnp.zeros((hidden_ref.shape[0], 1), F32)
    for at in range(0, width, width // 4):
        piece = hidden_ref[:, at : at + width // 4].astype(F32)
        square = square + jnp.sum(piece * piece, axis=1, keepdims=True)
    inv = lax.rsqrt(square / width + 1e-05)
    cot = cot_ref[...]
    places = []
    for s in range(shifts):
        x = lax.rem(here - s + shifts, shifts)
        for j in range(pairs):
            y = lax.rem(side + j, pairs)
            for ref, which in ((own_ref, core), (other_ref, 1 - core)):
                at = pl.multiple_of(((x * pairs + y) * 2 + which) * half, half)
                places.append((ref.at[s, j], pl.ds(at, half)))
    keys = jnp.zeros(keys_ref.shape, F32)
    for ref, columns in places:
        keys = keys + jnp.dot(hidden_ref[:, columns], ref[...], preferred_element_type=F32)
    keys = keys * inv
    keys_ref[...] = keys.astype(BF16)
    mean = jnp.sum(keys * cot.astype(F32), axis=1, keepdims=True) / width
    for ref, columns in places:
        value = lax.dot_general(cot, ref[...], (((1,), (1,)), ((), ())), preferred_element_type=F32)
        unit = hidden_ref[:, columns].astype(F32) * inv
        grad_ref[:, columns] = (inv * (value - unit * mean)).astype(BF16)


def total_kernel(scale, terms_ref, copies_ref):
    total = terms_ref[0].astype(F32)
    for i in range(1, terms_ref.shape[0]):
        total = total + terms_ref[i].astype(F32)
    total = (total if scale == 1 else total * scale).astype(BF16)
    for i in range(copies_ref.shape[0]):
        copies_ref[i] = total


def call(kernel, outs, specs, flops, moved, after=()):
    count = len(specs)

    def run(*refs):
        kernel(*refs[:count], *refs[count + len(after) :])

    made = pl.pallas_call(
        run,
        out_shape=outs,
        in_specs=specs + [pl.BlockSpec(memory_space=pl.ANY)] * len(after),
        out_specs=jax.tree.map(lambda _: VMEM, outs),
        compiler_params=PARAMS,
        cost_estimate=pl.CostEstimate(flops=flops, bytes_accessed=moved, transcendentals=0),
    )
    return lambda *operands: made(*operands, *after)


def tie(*values):
    return lax.optimization_barrier(values)


def body(hidden_in, norm_gain, key_codes, key_scales, key_cotangent):
    nx, nh, nl, nz, np, nc = (lax.axis_size(a) for a in ("x", "yh", "yl", "z", "zp", "c"))
    tok, width = hidden_in.shape
    rows, cols = key_codes.shape
    total_tokens = tok * nx * nh * nl * nz * np * nc
    half = rows // nc
    part = width // nx
    place = jnp.stack([lax.axis_index(a) for a in ("c", "x", "yh")]).astype(jnp.int32)
    scales, gain = key_scales.T, norm_gain[None]

    sent, mark = pl.pallas_call(
        prepare_kernel,
        out_shape=[shape((nx, tok, part + cols), BF16), shape((8, 1), F32)],
        in_specs=[HBM] * 2,
        out_specs=[HBM, VMEM],
        scratch_shapes=[
            pltpu.VMEM((nx, tok, part), BF16),
            pltpu.VMEM((tok, cols), BF16),
            pltpu.SemaphoreType.DMA((nx + 1,)),
            pltpu.SemaphoreType.DMA((2 * nx,)),
        ],
        compiler_params=pltpu.CompilerParams(vmem_limit_bytes=60 * 1024 * 1024),
        cost_estimate=pl.CostEstimate(flops=4 * tok * width, bytes_accessed=4 * tok * width, transcendentals=0),
    )(hidden_in, key_cotangent)
    got = lax.all_to_all(sent, "x", 0, 0)

    mine = call(gained_kernel, shape((half, cols), BF16), [SMEM, VMEM, VMEM, VMEM], half * cols, 4 * half * cols, [mark])(
        place, key_codes, scales, gain
    )
    mate = lax.ppermute(mine, "yh", SWAP)

    keep, send = call(
        product_kernel,
        [shape((nh, half, cols), F32), shape((nh, half, cols), BF16)],
        [SMEM, VMEM],
        2 * nx * tok * part * cols,
        2 * nx * tok * (part + cols) + 6 * nh * half * cols,
        [mate],
    )(place, got)
    product = (keep + lax.ppermute(send, "c", SWAP).astype(F32)).astype(BF16)
    pair = call(stack_kernel, shape((nh, half, cols), BF16), [VMEM] * 2, 0, 4 * nh * half * cols, [product])(mine, mate)

    quarter = half // nl
    eighth = quarter // np
    own = [pair] + [lax.ppermute(pair, "x", [(i, (i + s) % nx) for i in range(nx)]) for s in range(1, nx)]
    terms = lax.all_to_all(product.reshape(nh * nl * np, eighth, cols), ("yh", "yl", "zp"), 0, 0)
    copies = call(
        functools.partial(total_kernel, 1.0),
        shape((nz, eighth, cols), BF16),
        [VMEM],
        nh * nl * quarter * cols,
        2 * (nh * nl * np + nz) * eighth * cols,
    )(terms)
    own, mark = call(
        marked_stack_kernel,
        [shape((nx, nh, half, cols), BF16), shape((16, LANES), BF16)],
        [VMEM] * nx,
        0,
        4 * width * cols,
        [copies],
    )(*own)
    copies = call(
        functools.partial(total_kernel, float(total_tokens) ** -0.5),
        shape((nl * np, eighth, cols), BF16),
        [VMEM],
        nz * eighth * cols,
        2 * (nz + nl * np) * eighth * cols,
        [mark],
    )(lax.all_to_all(copies, "z", 0, 0))

    copies, own = tie(copies, own)

    whole = lax.all_to_all(copies, ("yl", "zp"), 0, 0).reshape(half, cols)
    other = lax.ppermute(own, "c", SWAP)
    beside = lax.ppermute(whole, "c", SWAP)
    mine = call(
        dots_kernel, shape((half // LANES, LANES), F32), [SMEM, VMEM, VMEM, VMEM], 2 * half * cols, 4 * half * cols
    )(place, whole, key_codes, scales)
    gain_part = call(
        pair_dots_kernel,
        shape((nx * nh, rows // LANES, LANES), F32),
        [SMEM, VMEM, VMEM, VMEM, VMEM],
        2 * half * cols,
        4 * half * cols,
    )(place, mine, beside, key_codes, scales)
    gain_gradient = lax.all_to_all(gain_part, ("x", "yh"), 0, 0).reshape(width)
    weight_grad = call(
        finish_kernel, shape((rows, cols), BF16), [SMEM, VMEM, VMEM, VMEM], rows * cols, 4 * rows * cols, [gain_part]
    )(place, whole, beside, gain)
    keys_out, input_gradient = call(
        tokens_kernel,
        [shape((tok, cols), BF16), shape((tok, width), BF16)],
        [SMEM, VMEM, VMEM, VMEM, VMEM],
        4 * tok * width * cols,
        4 * tok * width + 2 * width * cols,
        [gain_part],
    )(place, hidden_in, key_cotangent, own, other)
    gain_gradient, keys_out = tie(gain_gradient, keys_out)
    return (keys_out, input_gradient, weight_grad, gain_gradient)


def solution(mesh):
    axes = ("x", "yh", "yl", "z", "zp", "c")
    fine = Mesh(mesh.devices.reshape(4, 2, 4, 6, 2, 2), axes)
    tokens = P(axes, None)
    group = ("x", "yh")
    in_specs = (tokens, P(group), P(group, None), P(group, None), tokens)
    out_specs = (tokens, tokens, P(group, None), P())
    return jax.shard_map(body, mesh=fine, in_specs=in_specs, out_specs=out_specs, check_vma=False)
```
